512 devices in a mesh: wide: 32 (over z_lo, y, core), narrow: 16 (over x, z_hi).
Axes of the slice: x: 4, y: 4, z: 16 (z_hi: 4, z_lo: 4; z = z_hi * 4 + z_lo), core: 2. Of those that a mesh axis runs over, the one named last changes fastest.
Arguments:
- vectors: bfloat16 [3, 65536, 128], P(None, ('wide', 'narrow')), may hold values from -18 to 18
- hessian: bfloat16 [3, 3, 61, 65536], P(None, None, None, ('wide', 'narrow')), may hold values from -0.9 to 5.4
- neighbours: int32 [60, 65536], P(None, ('wide', 'narrow')), may hold values from 0 to 415
- halo_atoms: int32 [16384], P(('wide', 'narrow')), may hold values from 0 to 127
- labels: int32 [65536], P(('wide', 'narrow')), may hold values from 0 to 15
- masses: float32 [2, 16], replicated, may hold values from 1 to 32
- rotation: float32 [2, 128, 128], replicated, may hold values from -0.5 to 0.5
Outputs:
- gram: float32 [2, 128, 128], replicated
- rotated: bfloat16 [2, 3, 65536, 128], P(None, None, ('wide', 'narrow'))
The draws below stay inside these ranges and needn't reach their ends.
Inputs may be any that keep to these rules, and one draw needn't show every extreme that they name: `neighbours`: A row below 128 is a local atom of the domain; a row r at or above it is boundary atom (r - 128) % 32 of block (r - 128) // 32 in the 3x3 order of the steps.
All inputs are finite; a program needn't handle non-finite values.
Results may differ from the reference program's by a relative error of at most 0.003.
Values may be sent and summed in bfloat16 or wider, within the bound.
A program may use at most 64 MiB of HBM per device.

```python
import math
import jax
import jax.numpy as jnp
from jax import lax

NV = 128
NEIGH = 60
NISO = 16
A_DEV = 128
HALO_DEV = 32
ATOM_COUNT = 65536
HALOS = 16384
N_WIDE = 32
N_NARROW = 16


def draw_vectors(key, part):
    key_base = jax.random.fold_in(key, 11)
    key_rough = jax.random.fold_in(key, 12)
    shape = (3, ATOM_COUNT, NV)
    base = jnp.clip(jax.random.normal(key_base, shape, jnp.float32), -4.0, 4.0)
    ramp = jnp.exp(jnp.log(3.0) * jnp.arange(ATOM_COUNT, dtype=jnp.float32) / ATOM_COUNT)
    rough = jax.random.uniform(key_rough, (1, ATOM_COUNT, 1), jnp.float32, 0.5, 1.5)
    return (base * ramp[None, :, None] * rough).astype(jnp.bfloat16)


def draw_hessian(key, part):
    key_noise = jax.random.fold_in(key, 21)
    key_rough = jax.random.fold_in(key, 22)
    key_diag = jax.random.fold_in(key, 23)
    shape = (3, 3, NEIGH + 1, ATOM_COUNT)
    noise = jnp.clip(0.15 * jax.random.normal(key_noise, shape, jnp.float32), -0.6, 0.6)
    diag = jax.random.uniform(key_diag, (1, 1, 1, ATOM_COUNT), jnp.float32, 2.0, 4.0)
    rough = jax.random.uniform(key_rough, (1, 1, 1, ATOM_COUNT), jnp.float32, 0.5, 1.5)
    slot_zero = (jnp.arange(NEIGH + 1) == 0).astype(jnp.float32)[None, None, :, None]
    identity = jnp.eye(3, dtype=jnp.float32)[:, :, None, None]
    return (noise * rough + identity * slot_zero * diag).astype(jnp.bfloat16)


def set_ends(values, rng, smallest, top_value):
    shape = values.shape
    index_at = [jax.random.randint(jax.random.fold_in(rng, axis), (), 0, shape[axis]) for axis in range(len(shape))]
    values = values.at[tuple(index_at)].set(smallest)
    longest = shape.index(max(shape))
    index_at[longest] = (index_at[longest] + 1) % shape[longest]
    return values.at[tuple(index_at)].set(top_value)


def scatter_about(own_key, shape, spread, most, held_as=jnp.bfloat16):
    return jnp.clip(spread * jax.random.normal(own_key, shape, jnp.float32), -most, most).astype(held_as)


def setup_inputs(seed: int = 0) -> dict:
    key_list = jax.random.split(jax.random.key(seed), 8)
    vectors = draw_vectors(jax.random.fold_in(key_list[7], 71), 0)
    hessian = draw_hessian(jax.random.fold_in(key_list[7], 71), 0)
    neighbours = set_ends(jax.random.randint(key_list[2], (NEIGH, ATOM_COUNT), 0, A_DEV + 9 * HALO_DEV), jax.random.fold_in(key_list[2], 1), 0, (A_DEV + 9 * HALO_DEV) - 1).astype(jnp.int32)
    halo_atoms = set_ends(jax.random.randint(key_list[3], (HALOS,), 0, A_DEV), jax.random.fold_in(key_list[3], 1), 0, A_DEV - 1).astype(jnp.int32)
    labels = set_ends(jax.random.randint(key_list[4], (ATOM_COUNT,), 0, NISO), jax.random.fold_in(key_list[4], 1), 0, NISO - 1).astype(jnp.int32)
    masses = jnp.clip(jnp.exp(jax.random.uniform(key_list[5], (2, NISO), jnp.float32, math.log(1.0), math.log(32.0))), 1.0, 32.0)
    rotation = scatter_about(key_list[6], (2, NV, NV), NV ** -0.5, 0.5, jnp.float32)
    return {"vectors": vectors, "hessian": hessian, "neighbours": neighbours, "halo_atoms": halo_atoms, "labels": labels, "masses": masses, "rotation": rotation}


def reference(vectors, hessian, neighbours, halo_atoms, labels, masses, rotation):
    factors = lax.rsqrt(masses)[:, labels]
    vector_complete = vectors.astype(jnp.float32)
    scaled = jnp.concatenate([vector_complete * factors[0][None, :, None], vector_complete * factors[1][None, :, None]], axis=2).astype(jnp.bfloat16)

    def device_image(domain):
        wide_pos = domain // N_NARROW
        narrow_pos = domain % N_NARROW
        local = lax.dynamic_slice_in_dim(scaled, domain * A_DEV, A_DEV, 1)
        pieces = [local]
        for offset_a in range(3):
            for offset_b in range(3):
                src_wide = wide_pos + offset_a - 1
                src_narrow = narrow_pos + offset_b - 1
                inside = (src_wide >= 0) & (src_wide < N_WIDE) & (src_narrow >= 0) & (src_narrow < N_NARROW)
                source = (jnp.clip(src_wide, 0, N_WIDE - 1) * N_NARROW + jnp.clip(src_narrow, 0, N_NARROW - 1)).astype(jnp.int32)
                source_rows = lax.dynamic_slice_in_dim(halo_atoms, source * HALO_DEV, HALO_DEV) + source * A_DEV
                piece = jnp.take(scaled, source_rows.astype(jnp.int32), axis=1)
                pieces.append(jnp.where(inside, piece, jnp.zeros_like(piece)))
        extended = jnp.concatenate(pieces, axis=1)
        near = lax.dynamic_slice_in_dim(neighbours, domain * A_DEV, A_DEV, 1)
        blocks = lax.dynamic_slice_in_dim(hessian, domain * A_DEV, A_DEV, 3).astype(jnp.float32)
        picked = jnp.take(extended, near.reshape(-1), axis=1).reshape(3, NEIGH, A_DEV, 2 * NV).astype(jnp.float32)
        own_term = jnp.einsum('ija,jac->iac', blocks[:, :, 0], local.astype(jnp.float32), precision=lax.Precision.HIGHEST)
        far_term = jnp.einsum('ijka,jkac->iac', blocks[:, :, 1:], picked, precision=lax.Precision.HIGHEST)
        return own_term + far_term
    domains = jnp.arange(N_WIDE * N_NARROW, dtype=jnp.int32)
    images = lax.map(device_image, domains)
    product = jnp.moveaxis(images, 0, 1).reshape(3, ATOM_COUNT, 2 * NV)
    grams = []
    outputs = []
    for isotope_variant in range(2):
        hessian_image = product[:, :, isotope_variant * NV:(isotope_variant + 1) * NV] * factors[isotope_variant][None, :, None]
        gram_vector_block = jnp.einsum('eqv,eqh->vh', vector_complete, hessian_image, precision=lax.Precision.HIGHEST) / (3.0 * ATOM_COUNT)
        fresh_block = hessian_image - jnp.einsum('jyx,xs->jys', vector_complete, gram_vector_block, precision=lax.Precision.HIGHEST)
        turned_block = jnp.einsum('jyx,xs->jys', fresh_block, rotation[isotope_variant], precision=lax.Precision.HIGHEST)
        grams.append(gram_vector_block)
        outputs.append(turned_block.astype(jnp.bfloat16))
    return (jnp.stack(grams), jnp.stack(outputs))
```

```python
import functools

import jax
import jax.numpy as jnp
from jax import lax
from jax.experimental import pallas as pl
from jax.experimental.pallas import tpu as pltpu
from jax.sharding import PartitionSpec as P

MESH = pl.DeviceIdType.MESH
F32 = jnp.float32
BF16 = jnp.bfloat16
A = 128
H = 32
V = 128
K = 60
ROWS = A + 9 * H
NISO = 16
CENTRE = ROWS // 2


def dot(x, y, dims=((1,), (0,))):
    return lax.dot_general(x, y, (dims, ((), ())), preferred_element_type=F32)


def split(x):
    high = x.astype(BF16)
    return high, (x - high.astype(F32)).astype(BF16)


def iota(shape, dim):
    return lax.broadcasted_iota(jnp.int32, shape, dim)


def combine_duplicates(nbr_ref, hess_ref, nbr_pad, h_pad, nbr_x, h_x):
    nbr_pad[0:64, :] = jnp.full((64, A), -1.0, F32)
    nbr_pad[64:64 + K, :] = nbr_ref[...].astype(F32)
    nbr_pad[64 + K:128, :] = jnp.full((64 - K, A), -2.0, F32)
    for cj in range(9):
        h_pad[cj, 0:64, :] = jnp.zeros((64, A), F32)
        h_pad[cj, 64:64 + K, :] = hess_ref[cj // 3, cj % 3, 1:1 + K, :].astype(F32)
        h_pad[cj, 64 + K:128, :] = jnp.zeros((64 - K, A), F32)

    def eight_slots(m, _):
        first = 64 + 8 * m
        here = nbr_pad[pl.ds(first, 8), :]
        sums = tuple(h_pad[cj, pl.ds(first, 8), :] for cj in range(9))

        def eight_shifts(g, sums):
            for t in range(8):
                back = first - (8 * g + t + 1)
                same = nbr_pad[pl.ds(back, 8), :] == here
                sums = tuple(
                    s + jnp.where(same, h_pad[cj, pl.ds(back, 8), :], 0.0) for cj, s in enumerate(sums)
                )
            return sums

        sums = lax.fori_loop(0, m + 1, eight_shifts, sums)
        for t in range(8):
            nbr_x[8 * m + t] = jnp.broadcast_to(here[t:t + 1, :] - CENTRE, (16, A)).astype(BF16)
            for cj in range(9):
                h_x[cj, 8 * m + t] = jnp.broadcast_to(sums[cj][t:t + 1, :], (16, A)).astype(BF16)
        return 0

    lax.fori_loop(0, 8, eight_slots, 0)


def weight_rows(block, nbr_x, h_x):
    ids = (iota((16, A), 0) + (block * 32 - CENTRE)).astype(F32)
    low, high = ids.astype(BF16), (ids + 16.0).astype(BF16)
    zero = jnp.zeros((16, A), BF16)

    def ten_slots(g, sums):
        for t in range(10):
            k = g * 10 + t
            row = nbr_x[k]
            at_low, at_high = row == low, row == high
            out = []
            for cj in range(9):
                value = h_x[cj, k]
                out.append(jnp.where(at_low, value, sums[2 * cj]))
                out.append(jnp.where(at_high, value, sums[2 * cj + 1]))
            sums = tuple(out)
        return sums

    return lax.fori_loop(0, K // 10, ten_slots, (zero,) * 18)


def kernel(
    n_wide, n_narrow, per_z, z_high,
    vec_ref, hess_ref, nbr_ref, halo_ref, lab_ref, mass_ref, rot_ref,
    gram_ref, out_ref,
    x_ref, nbr_pad, h_pad, nbr_x, h_x, w_local, w_halo, wt_halo, g_ref, first_ref, part_ref, second_ref, turned_ref,
    halo_send, halo_recv, send_sem, recv_sem,
):
    p, q = lax.axis_index("wide"), lax.axis_index("narrow")
    z_low = n_wide // per_z
    n_x = n_narrow // z_high
    plane, along = per_z * n_x, z_low * z_high
    in_plane = lax.div(q, z_high) * per_z + lax.rem(p, per_z)
    in_z = lax.rem(q, z_high) * z_low + lax.div(p, per_z)

    def plane_device(index):
        return (
            lax.div(p, per_z) * per_z + lax.rem(index, per_z),
            lax.div(index, per_z) * z_high + lax.rem(q, z_high),
        )

    def z_device(index):
        return (
            lax.rem(index, z_low) * per_z + lax.rem(p, per_z),
            lax.div(q, z_high) * z_high + lax.div(index, z_low),
        )

    has = {"up": p > 0, "down": p < n_wide - 1, "left": q > 0, "right": q < n_narrow - 1}
    where = {"up": (p - 1, q), "down": (p + 1, q), "left": (p, q - 1), "right": (p, q + 1)}

    for name, index in (("left", 0), ("right", 2)):
        @pl.when(jnp.logical_not(has[name]))
        def _():
            x_ref[1, index] = jnp.zeros((4, H, V), BF16)
    for name, index in (("up", 0), ("down", 2)):
        @pl.when(jnp.logical_not(has[name]))
        def _():
            x_ref[index] = jnp.zeros((3, 4, H, V), BF16)

    barrier = pltpu.get_barrier_semaphore()

    def greet(device):
        pl.semaphore_signal(barrier, inc=1, device_id=device, device_id_type=MESH)

    for name in has:
        @pl.when(has[name])
        def _():
            greet(where[name])

    def greet_plane(d, _):
        greet(plane_device(lax.rem(in_plane + d, plane)))
        return 0

    def greet_z(d, _):
        greet(z_device(lax.rem(in_z + d, along)))
        return 0

    lax.fori_loop(1, plane, greet_plane, 0)
    lax.fori_loop(1, along, greet_z, 0)

    masses = mass_ref[...]
    roots = lax.rsqrt(masses)
    roots = roots * (1.5 - 0.5 * masses * roots * roots)
    pick = lax.rem(iota((A, NISO), 0), NISO) == iota((A, NISO), 1)
    group = iota((A, V), 0)
    table = []
    for iso in range(2):
        column = jnp.sum(jnp.where(pick, roots[iso:iso + 1, :], 0.0), axis=1, keepdims=True)
        full = jnp.broadcast_to(column, (A, V))
        one = full.astype(BF16).astype(F32)
        two = (full - one).astype(BF16).astype(F32)
        three = full - one - two
        table.append(
            jnp.where(group < 16, one, jnp.where(group < 32, two, jnp.where(group < 48, three, 0.0))).astype(BF16)
        )
    table = jnp.concatenate(table, axis=1)
    classes = jnp.where(
        (lax.rem(group, NISO) == lab_ref[...]) & (group < 3 * NISO), 1.0, 0.0
    ).T.astype(BF16)
    factors = dot(classes, table)

    boundary = jnp.where(iota((A, H), 0) == halo_ref[...], 1.0, 0.0).astype(BF16)
    for j in range(3):
        x_ref[1, 1, j] = dot(boundary, vec_ref[j], ((0,), (0,))).astype(BF16)
    x_ref[1, 1, 3] = dot(boundary, classes, ((0,), (0,))).astype(BF16)

    greetings = plane + along - 2
    for name in has:
        greetings = greetings + has[name].astype(jnp.int32)
    pl.semaphore_wait(barrier, greetings)

    def halo_copy(j, at, name):
        number = at[0] * 3 + at[1]
        return pltpu.make_async_remote_copy(
            src_ref=x_ref.at[1, j], dst_ref=x_ref.at[at[0], at[1]],
            send_sem=halo_send.at[number], recv_sem=halo_recv.at[number],
            device_id=where[name], device_id_type=MESH,
        )

    to_right, to_left = halo_copy(1, (1, 0), "right"), halo_copy(1, (1, 2), "left")
    to_down = [halo_copy(j, (0, j), "down") for j in range(3)]
    to_up = [halo_copy(j, (2, j), "up") for j in range(3)]
    pl.when(has["right"])(to_right.start)
    pl.when(has["left"])(to_left.start)
    pl.when(has["down"])(to_down[1].start)
    pl.when(has["up"])(to_up[1].start)

    vectors = [vec_ref[j] for j in range(3)]
    stacked = vec_ref[...].reshape(3 * A, V)
    turned = stacked.astype(F32).T.astype(BF16)

    combine_duplicates(nbr_ref, hess_ref, nbr_pad, h_pad, nbr_x, h_x)

    def local_block(block, _):
        rows = weight_rows(block, nbr_x, h_x)
        for cj in range(9):
            at = pl.multiple_of(block * 32, 32)
            w_local[cj, pl.ds(at, 16), :] = rows[2 * cj]
            w_local[cj, pl.ds(pl.multiple_of(at + 16, 16), 16), :] = rows[2 * cj + 1]
        return 0

    lax.fori_loop(0, A // 32, local_block, 0)

    def halo_block(block, _):
        rows = weight_rows(block + A // 32, nbr_x, h_x)
        for cj in range(9):
            at = pl.multiple_of((cj % 3) * 9 * H + block * 32, 32)
            w_halo[cj // 3, pl.ds(at, 16), :] = rows[2 * cj]
            w_halo[cj // 3, pl.ds(pl.multiple_of(at + 16, 16), 16), :] = rows[2 * cj + 1]
        return 0

    lax.fori_loop(0, 5, halo_block, 0)

    pl.when(has["left"])(to_right.wait_recv)
    pl.when(has["down"])(to_down[0].start)
    pl.when(has["up"])(to_up[0].start)
    pl.when(has["right"])(to_left.wait_recv)
    pl.when(has["down"])(to_down[2].start)
    pl.when(has["up"])(to_up[2].start)

    lax.fori_loop(5, 9, halo_block, 0)

    own = iota((A, A), 0) == iota((A, A), 1)
    scaled = [
        (jnp.concatenate([v.astype(F32)] * 2, axis=1) * factors).astype(BF16) for v in vectors
    ]
    scaled = jnp.concatenate(scaled, axis=0)
    products = []
    for c in range(3):
        diagonal = jnp.concatenate(
            [jnp.where(own, hess_ref[c, j, 0:1, :].astype(F32), 0.0).astype(BF16) for j in range(3)], axis=1
        )
        near = jnp.concatenate([w_local[c * 3 + j].T for j in range(3)], axis=1)
        products.append(dot(diagonal, scaled) + dot(near, scaled))
        wt_halo[c * A:(c + 1) * A, :] = w_halo[c].T

    for name, copies in (("up", to_down), ("down", to_up)):
        @pl.when(has[name])
        def _():
            for copy in copies:
                copy.wait_recv()

    outer = x_ref[...].reshape(9, 4, H, V)
    far_factors = dot(outer[:, 3].reshape(9 * H, V), table)
    far = [
        (jnp.concatenate([outer[:, j].reshape(9 * H, V).astype(F32)] * 2, axis=1) * far_factors).astype(BF16)
        for j in range(3)
    ]
    product = jnp.concatenate(products, axis=0) + dot(wt_halo[...], jnp.concatenate(far, axis=0))
    image = product * jnp.concatenate([factors] * 3, axis=0)
    image_high, image_low = split(image)
    gram = dot(turned, image_high) + dot(turned, image_low)
    rows = 2 * V // plane
    for iso in range(2):
        g_ref[iso * (plane // 2):(iso + 1) * (plane // 2)] = gram[:, iso * V:(iso + 1) * V].reshape(plane // 2, rows, V)

    def scatter(d, _):
        target = lax.rem(in_plane + d, plane)
        pltpu.make_async_remote_copy(
            src_ref=g_ref.at[target], dst_ref=first_ref.at[plane - 1 - d],
            send_sem=send_sem.at[0], recv_sem=recv_sem.at[0],
            device_id=plane_device(target), device_id_type=MESH,
        ).start()
        return 0

    lax.fori_loop(1, plane, scatter, 0)

    def arrived(ref, number):
        pltpu.make_async_copy(ref, ref, recv_sem.at[number]).wait()

    def sent(ref, number):
        pltpu.make_async_copy(ref, ref, send_sem.at[number]).wait()

    rotations = [split(rot_ref[iso]) for iso in range(2)]
    for iso in range(2):
        high, low = image_high[:, iso * V:(iso + 1) * V], image_low[:, iso * V:(iso + 1) * V]
        r_high, r_low = rotations[iso]
        turned_ref[iso] = dot(high, r_high) + (dot(high, r_low) + dot(low, r_high))

    arrived(first_ref, 0)
    part_ref[0] = g_ref[in_plane] + jnp.sum(first_ref[...], axis=0)

    def exchange(d, _):
        target = lax.rem(in_z + d, along)
        pltpu.make_async_remote_copy(
            src_ref=part_ref.at[0], dst_ref=second_ref.at[along - 1 - d],
            send_sem=send_sem.at[1], recv_sem=recv_sem.at[1],
            device_id=z_device(target), device_id_type=MESH,
        ).start()
        return 0

    lax.fori_loop(1, along, exchange, 0)
    arrived(second_ref, 1)
    atoms_all = 3.0 * A * n_wide * n_narrow
    total = (part_ref[0] + jnp.sum(second_ref[...], axis=0)) / atoms_all
    sent(first_ref, 0)
    final_ref = part_ref.at[1]
    final_ref[...] = total

    def gather(d, _):
        target = lax.rem(in_plane + d, plane)
        pltpu.make_async_remote_copy(
            src_ref=final_ref, dst_ref=gram_ref.at[in_plane],
            send_sem=send_sem.at[2], recv_sem=recv_sem.at[2],
            device_id=plane_device(target), device_id_type=MESH,
        ).start()
        return 0

    lax.fori_loop(1, plane, gather, 0)
    gram_ref[in_plane] = total
    arrived(first_ref, 2)
    for iso in range(2):
        whole = gram_ref[iso * (plane // 2):(iso + 1) * (plane // 2)].reshape(V, V)
        high, low = split(whole)
        r_high, r_low = rotations[iso]
        m_high, m_low = split(dot(high, r_high) + (dot(high, r_low) + dot(low, r_high)))
        out_ref[iso] = (
            turned_ref[iso] - (dot(stacked, m_high) + dot(stacked, m_low))
        ).astype(BF16).reshape(3, A, V)

    sent(second_ref, 1)
    sent(first_ref, 2)
    pl.when(has["right"])(to_right.wait_send)
    pl.when(has["left"])(to_left.wait_send)
    for name, copies in (("down", to_down), ("up", to_up)):
        @pl.when(has[name])
        def _():
            for copy in copies:
                copy.wait_send()


def local(n_wide, n_narrow, per_z, z_high, vectors, hessian, neighbours, halo_atoms, labels, masses, rotation):
    plane = per_z * (n_narrow // z_high)
    along = (n_wide // per_z) * z_high
    rows = 2 * V // plane
    vmem = pl.BlockSpec(memory_space=pltpu.VMEM)
    gram, rotated = pl.pallas_call(
        functools.partial(kernel, n_wide, n_narrow, per_z, z_high),
        out_shape=(
            jax.ShapeDtypeStruct((plane, rows, V), F32),
            jax.ShapeDtypeStruct((2, 3, A, V), BF16),
        ),
        in_specs=[vmem] * 7,
        out_specs=(vmem, vmem),
        scratch_shapes=[
            pltpu.VMEM((3, 3, 4, H, V), BF16),
            pltpu.VMEM((128, A), F32),
            pltpu.VMEM((9, 128, A), F32),
            pltpu.VMEM((64, 16, A), BF16),
            pltpu.VMEM((9, 64, 16, A), BF16),
            pltpu.VMEM((9, A, A), BF16),
            pltpu.VMEM((3, 27 * H, A), BF16),
            pltpu.VMEM((3 * A, 27 * H), BF16),
            pltpu.VMEM((plane, rows, V), F32),
            pltpu.VMEM((plane - 1, rows, V), F32),
            pltpu.VMEM((2, rows, V), F32),
            pltpu.VMEM((along - 1, rows, V), F32),
            pltpu.VMEM((2, 3 * A, V), F32),
            pltpu.SemaphoreType.DMA((9,)),
            pltpu.SemaphoreType.DMA((9,)),
            pltpu.SemaphoreType.DMA((3,)),
            pltpu.SemaphoreType.DMA((3,)),
        ],
        compiler_params=pltpu.CompilerParams(
            collective_id=0, has_side_effects=True, vmem_limit_bytes=32 * 1024 * 1024
        ),
    )(vectors, hessian, neighbours, halo_atoms.reshape(1, H), labels.reshape(1, A), masses, rotation)
    return gram.reshape(2, V, V), rotated


def solution(mesh):
    n_wide, n_narrow = mesh.shape["wide"], mesh.shape["narrow"]
    per_z = n_wide // 4 if n_wide >= 16 else n_wide // 2
    z_high = 4 if n_narrow >= 16 else n_narrow // 2
    spread = ("wide", "narrow")
    return jax.shard_map(
        functools.partial(local, n_wide, n_narrow, per_z, z_high),
        mesh=mesh,
        in_specs=(
            P(None, spread, None),
            P(None, None, None, spread),
            P(None, spread),
            P(spread),
            P(spread),
            P(),
            P(),
        ),
        out_specs=(P(), P(None, None, spread, None)),
        check_vma=False,
    )
```

```python
import functools

import jax
import jax.numpy as jnp
from jax import lax
from jax.experimental import pallas as pl
from jax.experimental.pallas import tpu as pltpu
from jax.sharding import PartitionSpec as P

MESH = pl.DeviceIdType.MESH
F32 = jnp.float32
BF16 = jnp.bfloat16
A = 128
H = 32
V = 128
K = 60
ROWS = A + 9 * H
NISO = 16
CORNERS, EDGES = (0, 2, 6, 8), (1, 3, 4, 5, 7)
PAY = 3 * H + H // 2
CENTRE = ROWS // 2


def dot(x, y, dims=((1,), (0,))):
    return lax.dot_general(x, y, (dims, ((), ())), preferred_element_type=F32)


def split(x):
    high = x.astype(BF16)
    return high, (x - high.astype(F32)).astype(BF16)


def iota(shape, dim):
    return lax.broadcasted_iota(jnp.int32, shape, dim)


def combine_duplicates(nbr_ref, hess_ref, nbr_pad, h_pad, nbr_x, h_x):
    nbr_pad[0:64, :] = jnp.full((64, A), -1.0, F32)
    nbr_pad[64:64 + K, :] = nbr_ref[...].astype(F32)
    nbr_pad[64 + K:128, :] = jnp.full((64 - K, A), -2.0, F32)
    for cj in range(9):
        h_pad[cj, 0:64, :] = jnp.zeros((64, A), F32)
        h_pad[cj, 64:64 + K, :] = hess_ref[cj // 3, cj % 3, 1:1 + K, :].astype(F32)
        h_pad[cj, 64 + K:128, :] = jnp.zeros((64 - K, A), F32)

    def eight_slots(m, _):
        first = 64 + 8 * m
        here = nbr_pad[pl.ds(first, 8), :]
        sums = tuple(h_pad[cj, pl.ds(first, 8), :] for cj in range(9))

        def eight_shifts(g, sums):
            for t in range(8):
                back = first - (8 * g + t + 1)
                same = nbr_pad[pl.ds(back, 8), :] == here
                sums = tuple(
                    s + jnp.where(same, h_pad[cj, pl.ds(back, 8), :], 0.0) for cj, s in enumerate(sums)
                )
            return sums

        sums = lax.fori_loop(0, m + 1, eight_shifts, sums)
        for t in range(8):
            nbr_x[8 * m + t] = jnp.broadcast_to(here[t:t + 1, :] - CENTRE, (16, A)).astype(BF16)
            for cj in range(9):
                h_x[cj, 8 * m + t] = jnp.broadcast_to(sums[cj][t:t + 1, :], (16, A)).astype(BF16)
        return 0

    lax.fori_loop(0, 8, eight_slots, 0)


def weight_rows(block, nbr_x, h_x):
    ids = (iota((16, A), 0) + (block * 32 - CENTRE)).astype(F32)
    low, high = ids.astype(BF16), (ids + 16.0).astype(BF16)
    zero = jnp.zeros((16, A), BF16)

    def ten_slots(g, sums):
        for t in range(10):
            k = g * 10 + t
            row = nbr_x[k]
            at_low, at_high = row == low, row == high
            out = []
            for cj in range(9):
                value = h_x[cj, k]
                out.append(jnp.where(at_low, value, sums[2 * cj]))
                out.append(jnp.where(at_high, value, sums[2 * cj + 1]))
            sums = tuple(out)
        return sums

    return lax.fori_loop(0, K // 10, ten_slots, (zero,) * 18)


def kernel(
    n_wide, n_narrow, per_z, z_high,
    vec_in, hess_in, nbr_in, halo_in, lab_in, mass_in, rot_in,
    gram_ref, out_ref,
    vec_ref, hess_ref, nbr_ref, halo_ref, lab_ref, mass_ref, rot_ref,
    x_ref, nbr_pad, h_pad, nbr_x, h_x, w_local, w_halo, wt_halo, g_ref, first_ref, part_ref, second_ref, turned_ref,
    load_sem, halo_send, halo_recv, send_sem, recv_sem, relay_sem,
):
    p, q = lax.axis_index("wide"), lax.axis_index("narrow")
    z_low = n_wide // per_z
    n_x = n_narrow // z_high
    plane, along = per_z * n_x, z_low * z_high
    in_plane = lax.div(q, z_high) * per_z + lax.rem(p, per_z)
    in_z = lax.rem(q, z_high) * z_low + lax.div(p, per_z)

    def plane_device(index):
        return (
            lax.div(p, per_z) * per_z + lax.rem(index, per_z),
            lax.div(index, per_z) * z_high + lax.rem(q, z_high),
        )

    def z_device(index):
        return (
            lax.rem(index, z_low) * per_z + lax.rem(p, per_z),
            lax.div(q, z_high) * z_high + lax.div(index, z_low),
        )

    has = {"up": p > 0, "down": p < n_wide - 1, "left": q > 0, "right": q < n_narrow - 1}
    where = {"up": (p - 1, q), "down": (p + 1, q), "left": (p, q - 1), "right": (p, q + 1)}

    for name, index in (("left", 0), ("right", 2)):
        @pl.when(jnp.logical_not(has[name]))
        def _():
            x_ref[1, index] = jnp.zeros((PAY, V), BF16)
    for name, index in (("up", 0), ("down", 2)):
        @pl.when(jnp.logical_not(has[name]))
        def _():
            x_ref[index] = jnp.zeros((3, PAY, V), BF16)

    barrier = pltpu.get_barrier_semaphore()

    def greet(device):
        pl.semaphore_signal(barrier, inc=1, device_id=device, device_id_type=MESH)

    for name in has:
        @pl.when(has[name])
        def _():
            greet(where[name])

    def greet_plane(d, _):
        greet(plane_device(lax.rem(in_plane + d, plane)))
        return 0

    def greet_z(d, _):
        greet(z_device(lax.rem(in_z + d, along)))
        return 0

    reach = along // 4
    lax.fori_loop(1, reach + 1, greet_z, 0)
    lax.fori_loop(along - reach, along, greet_z, 0)
    lax.fori_loop(1, plane, greet_plane, 0)

    loads = [
        pltpu.make_async_copy(source, target, load_sem.at[number])
        for number, (source, target) in enumerate((
            (halo_in, halo_ref), (lab_in, lab_ref), (mass_in, mass_ref), (vec_in, vec_ref),
            (nbr_in, nbr_ref), (hess_in, hess_ref), (rot_in, rot_ref),
        ))
    ]
    for load in loads:
        load.start()
    for load in loads[:4]:
        load.wait()

    masses = mass_ref[...]
    roots = lax.rsqrt(masses)
    roots = roots * (1.5 - 0.5 * masses * roots * roots)
    pick = lax.rem(iota((A, NISO), 0), NISO) == iota((A, NISO), 1)
    group = iota((A, V), 0)
    table = []
    for iso in range(2):
        column = jnp.sum(jnp.where(pick, roots[iso:iso + 1, :], 0.0), axis=1, keepdims=True)
        full = jnp.broadcast_to(column, (A, V))
        one = full.astype(BF16).astype(F32)
        two = (full - one).astype(BF16).astype(F32)
        three = full - one - two
        table.append(
            jnp.where(group < 16, one, jnp.where(group < 32, two, jnp.where(group < 48, three, 0.0))).astype(BF16)
        )
    table = jnp.concatenate(table, axis=1)
    table_two = jnp.concatenate([jnp.zeros((V // 2, 2 * V), BF16), table[:V // 2]], axis=0)
    half = lax.rem(group, V // 2)
    classes = jnp.where(
        (lax.rem(group, NISO) == lab_ref[...]) & (half < 3 * NISO), 1.0, 0.0
    ).T.astype(BF16)
    factors = dot(classes, table)

    boundary = jnp.where(iota((A, H), 0) == halo_ref[...], 1.0, 0.0).astype(BF16)
    for j in range(3):
        x_ref[1, 1, j * H:(j + 1) * H, :] = dot(boundary, vec_ref[j], ((0,), (0,))).astype(BF16)
    chosen = dot(boundary, classes, ((0,), (0,)))
    x_ref[1, 1, 3 * H:, :] = jnp.where(
        iota((H // 2, V), 1) < V // 2, chosen[:H // 2], chosen[H // 2:]
    ).astype(BF16)

    for load in loads[4:]:
        load.wait()
    vectors = [vec_ref[j] for j in range(3)]
    stacked = vec_ref[...].reshape(3 * A, V)
    turned = stacked.astype(F32).T.astype(BF16)

    combine_duplicates(nbr_ref, hess_ref, nbr_pad, h_pad, nbr_x, h_x)

    def local_block(block, _):
        rows = weight_rows(block, nbr_x, h_x)
        for cj in range(9):
            at = pl.multiple_of(block * 32, 32)
            w_local[cj, pl.ds(at, 16), :] = rows[2 * cj]
            w_local[cj, pl.ds(pl.multiple_of(at + 16, 16), 16), :] = rows[2 * cj + 1]
        return 0

    lax.fori_loop(0, A // 32, local_block, 0)

    greetings = plane - 1 + 2 * reach
    for name in has:
        greetings = greetings + has[name].astype(jnp.int32)
    pl.semaphore_wait(barrier, greetings)

    def halo_copy(j, at, name):
        number = at[0] * 3 + at[1]
        return pltpu.make_async_remote_copy(
            src_ref=x_ref.at[1, j], dst_ref=x_ref.at[at[0], at[1]],
            send_sem=halo_send.at[number], recv_sem=halo_recv.at[number],
            device_id=where[name], device_id_type=MESH,
        )

    to_right, to_left = halo_copy(1, (1, 0), "right"), halo_copy(1, (1, 2), "left")
    to_down = [halo_copy(j, (0, j), "down") for j in range(3)]
    to_up = [halo_copy(j, (2, j), "up") for j in range(3)]
    pl.when(has["right"])(to_right.start)
    pl.when(has["left"])(to_left.start)
    pl.when(has["down"])(to_down[1].start)
    pl.when(has["up"])(to_up[1].start)

    for d in (reach, along - reach):
        pl.semaphore_signal(relay_sem, inc=1, device_id=z_device(lax.rem(in_z + d, along)), device_id_type=MESH)

    def halo_block(block, _):
        rows = weight_rows(block + A // 32, nbr_x, h_x)
        for cj in range(9):
            at = (cj % 3) * H
            w_halo[cj // 3, block, at:at + 16, :] = rows[2 * cj]
            w_halo[cj // 3, block, at + 16:at + 32, :] = rows[2 * cj + 1]
        return 0

    lax.fori_loop(0, 8, halo_block, 0)

    pl.when(has["left"])(to_right.wait_recv)
    pl.when(has["down"])(to_down[0].start)
    pl.when(has["up"])(to_up[0].start)
    pl.when(has["right"])(to_left.wait_recv)
    pl.when(has["down"])(to_down[2].start)
    pl.when(has["up"])(to_up[2].start)

    lax.fori_loop(8, 9, halo_block, 0)

    own = iota((A, A), 0) == iota((A, A), 1)
    scaled = [
        (jnp.concatenate([v.astype(F32)] * 2, axis=1) * factors).astype(BF16) for v in vectors
    ]
    scaled = jnp.concatenate(scaled, axis=0)
    products = []
    for c in range(3):
        diagonal = jnp.concatenate(
            [jnp.where(own, hess_ref[c, j, 0:1, :].astype(F32), 0.0).astype(BF16) for j in range(3)], axis=1
        )
        near = jnp.concatenate([w_local[c * 3 + j].T for j in range(3)], axis=1)
        products.append(dot(diagonal, scaled) + dot(near, scaled))
        wt_halo[c * A:(c + 1) * A, :] = jnp.concatenate([w_halo[c, b] for b in CORNERS], axis=0).T

    def far_rows(blocks):
        out = []
        for b in blocks:
            block = x_ref[b // 3, b % 3]
            packed = block[3 * H:]
            scale = jnp.concatenate([dot(packed, table), dot(packed, table_two)], axis=0)
            for j in range(3):
                rows = block[j * H:(j + 1) * H].astype(F32)
                out.append((jnp.concatenate([rows, rows], axis=1) * scale).astype(BF16))
        return jnp.concatenate(out, axis=0)

    for name, copies in (("up", to_down), ("down", to_up)):
        pl.when(has[name])(copies[1].wait_recv)
    edge_rows = far_rows(EDGES)
    for c in range(3):
        edges = jnp.concatenate([w_halo[c, b] for b in EDGES], axis=0).T
        products[c] += dot(edges, edge_rows)
    early = jnp.concatenate(products, axis=0)
    all_factors = jnp.concatenate([factors] * 3, axis=0)

    for name, copies in (("up", to_down), ("down", to_up)):
        @pl.when(has[name])
        def _():
            copies[0].wait_recv()
            copies[2].wait_recv()

    product = early + dot(wt_halo[...], far_rows(CORNERS))
    image = product * all_factors
    image_high, image_low = split(image)
    gram = dot(turned, image_high) + dot(turned, image_low)
    rows = 2 * V // plane
    for iso in range(2):
        g_ref[iso * (plane // 2):(iso + 1) * (plane // 2)] = gram[:, iso * V:(iso + 1) * V].reshape(plane // 2, rows, V)

    def scatter(d):
        target = lax.rem(in_plane + d, plane)
        pltpu.make_async_remote_copy(
            src_ref=g_ref.at[target], dst_ref=first_ref.at[plane - 1 - d],
            send_sem=send_sem.at[0], recv_sem=recv_sem.at[0],
            device_id=plane_device(target), device_id_type=MESH,
        ).start()

    def ring(distance, size):
        return min(distance % size, -distance % size)

    plane_order = sorted(
        range(1, plane), key=lambda d: -ring(d // per_z, n_x) - ring(d // 2 % (per_z // 2), per_z // 2)
    )
    z_order = sorted(range(1, along), key=lambda d: -ring(d, along))
    for d in plane_order:
        scatter(d)

    def arrived(ref, number):
        pltpu.make_async_copy(ref, ref, recv_sem.at[number]).wait()

    def sent(ref, number):
        pltpu.make_async_copy(ref, ref, send_sem.at[number]).wait()

    rotations = [split(rot_ref[iso]) for iso in range(2)]
    for iso in range(2):
        high, low = image_high[:, iso * V:(iso + 1) * V], image_low[:, iso * V:(iso + 1) * V]
        r_high, r_low = rotations[iso]
        turned_ref[iso] = dot(high, r_high) + (dot(high, r_low) + dot(low, r_high))

    arrived(first_ref, 0)
    part_ref[0] = g_ref[in_plane] + jnp.sum(first_ref[...], axis=0)

    def exchange(d):
        target = lax.rem(in_z + d, along)
        pltpu.make_async_remote_copy(
            src_ref=part_ref.at[0], dst_ref=second_ref.at[along - 1 - d],
            send_sem=send_sem.at[1], recv_sem=recv_sem.at[1],
            device_id=z_device(target), device_id_type=MESH,
        ).start()

    pl.semaphore_wait(relay_sem, 2)
    for d in z_order:
        exchange(d)
    arrived(second_ref, 1)
    atoms_all = 3.0 * A * n_wide * n_narrow
    total = (part_ref[0] + jnp.sum(second_ref[...], axis=0)) / atoms_all
    sent(first_ref, 0)
    final_ref = part_ref.at[1]
    final_ref[...] = total

    def gather(d):
        target = lax.rem(in_plane + d, plane)
        pltpu.make_async_remote_copy(
            src_ref=final_ref, dst_ref=gram_ref.at[in_plane],
            send_sem=send_sem.at[2], recv_sem=recv_sem.at[2],
            device_id=plane_device(target), device_id_type=MESH,
        ).start()

    for d in plane_order:
        gather(d)
    gram_ref[in_plane] = total
    arrived(first_ref, 2)
    for iso in range(2):
        whole = gram_ref[iso * (plane // 2):(iso + 1) * (plane // 2)].reshape(V, V)
        high, low = split(whole)
        r_high, r_low = rotations[iso]
        m_high, m_low = split(dot(high, r_high) + (dot(high, r_low) + dot(low, r_high)))
        out_ref[iso] = (
            turned_ref[iso] - (dot(stacked, m_high) + dot(stacked, m_low))
        ).astype(BF16).reshape(3, A, V)

    sent(second_ref, 1)
    sent(first_ref, 2)
    pl.when(has["right"])(to_right.wait_send)
    pl.when(has["left"])(to_left.wait_send)
    for name, copies in (("down", to_down), ("up", to_up)):
        @pl.when(has[name])
        def _():
            for copy in copies:
                copy.wait_send()


def local(n_wide, n_narrow, per_z, z_high, vectors, hessian, neighbours, halo_atoms, labels, masses, rotation):
    plane = per_z * (n_narrow // z_high)
    along = (n_wide // per_z) * z_high
    rows = 2 * V // plane
    vmem = pl.BlockSpec(memory_space=pltpu.VMEM)
    gram, rotated = pl.pallas_call(
        functools.partial(kernel, n_wide, n_narrow, per_z, z_high),
        out_shape=(
            pltpu.VMEM((plane, rows, V), F32),
            pltpu.VMEM((2, 3, A, V), BF16),
        ),
        in_specs=[pl.BlockSpec(memory_space=pltpu.HBM)] * 7,
        out_specs=(vmem, vmem),
        scratch_shapes=[
            pltpu.VMEM((3, A, V), BF16),
            pltpu.VMEM((3, 3, 1 + K, A), BF16),
            pltpu.VMEM((K, A), jnp.int32),
            pltpu.VMEM((1, H), jnp.int32),
            pltpu.VMEM((1, A), jnp.int32),
            pltpu.VMEM((2, NISO), F32),
            pltpu.VMEM((2, V, V), F32),
            pltpu.VMEM((3, 3, PAY, V), BF16),
            pltpu.VMEM((128, A), F32),
            pltpu.VMEM((9, 128, A), F32),
            pltpu.VMEM((64, 16, A), BF16),
            pltpu.VMEM((9, 64, 16, A), BF16),
            pltpu.VMEM((9, A, A), BF16),
            pltpu.VMEM((3, 9, 3 * H, A), BF16),
            pltpu.VMEM((3 * A, 12 * H), BF16),
            pltpu.VMEM((plane, rows, V), F32),
            pltpu.VMEM((plane - 1, rows, V), F32),
            pltpu.VMEM((2, rows, V), F32),
            pltpu.VMEM((along - 1, rows, V), F32),
            pltpu.VMEM((2, 3 * A, V), F32),
            pltpu.SemaphoreType.DMA((7,)),
            pltpu.SemaphoreType.DMA((9,)),
            pltpu.SemaphoreType.DMA((9,)),
            pltpu.SemaphoreType.DMA((3,)),
            pltpu.SemaphoreType.DMA((3,)),
            pltpu.SemaphoreType.REGULAR,
        ],
        compiler_params=pltpu.CompilerParams(
            collective_id=0, has_side_effects=True, vmem_limit_bytes=60 * 1024 * 1024
        ),
    )(vectors, hessian, neighbours, halo_atoms.reshape(1, H), labels.reshape(1, A), masses, rotation)
    return gram.reshape(2, V, V), rotated


def solution(mesh):
    n_wide, n_narrow = mesh.shape["wide"], mesh.shape["narrow"]
    per_z = n_wide // 4 if n_wide >= 16 else n_wide // 2
    z_high = 4 if n_narrow >= 16 else n_narrow // 2
    spread = ("wide", "narrow")
    return jax.shard_map(
        functools.partial(local, n_wide, n_narrow, per_z, z_high),
        mesh=mesh,
        in_specs=(
            P(None, spread, None),
            P(None, None, None, spread),
            P(None, spread),
            P(spread),
            P(spread),
            P(),
            P(),
        ),
        out_specs=(P(), P(None, None, spread, None)),
        check_vma=False,
    )
```

```python
import functools

import jax
import jax.numpy as jnp
from jax import lax
from jax.experimental import pallas as pl
from jax.experimental.pallas import tpu as pltpu
from jax.sharding import PartitionSpec as P

MESH = pl.DeviceIdType.MESH
F32 = jnp.float32
BF16 = jnp.bfloat16
A = 128
H = 32
V = 128
K = 60
UNROLL = 30
ROWS = A + 9 * H
NISO = 16
CORNERS, EDGES = (0, 2, 6, 8), (1, 3, 4, 5, 7)
PAY = 3 * H + H // 2
CENTRE = ROWS // 2


def dot(x, y, dims=((1,), (0,))):
    return lax.dot_general(x, y, (dims, ((), ())), preferred_element_type=F32)


def split(x):
    high = x.astype(BF16)
    return high, (x - high.astype(F32)).astype(BF16)


def iota(shape, dim):
    return lax.broadcasted_iota(jnp.int32, shape, dim)


def combine_duplicates(nbr_ref, hess_ref, nbr_pad, h_pad, nbr_x, h_x):
    nbr_pad[0:64, :] = jnp.full((64, A), -1.0, F32)
    nbr_pad[64:64 + K, :] = nbr_ref[...].astype(F32)
    nbr_pad[64 + K:128, :] = jnp.full((64 - K, A), -2.0, F32)
    for cj in range(9):
        h_pad[cj, 0:64, :] = jnp.zeros((64, A), F32)
        h_pad[cj, 64:64 + K, :] = hess_ref[cj // 3, cj % 3, 1:1 + K, :].astype(F32)
        h_pad[cj, 64 + K:128, :] = jnp.zeros((64 - K, A), F32)

    def eight_slots(m, _):
        first = 64 + 8 * m
        here = nbr_pad[pl.ds(first, 8), :]
        sums = tuple(h_pad[cj, pl.ds(first, 8), :] for cj in range(9))

        def eight_shifts(g, sums):
            for t in range(8):
                back = first - (8 * g + t + 1)
                same = nbr_pad[pl.ds(back, 8), :] == here
                sums = tuple(
                    s + jnp.where(same, h_pad[cj, pl.ds(back, 8), :], 0.0) for cj, s in enumerate(sums)
                )
            return sums

        sums = lax.fori_loop(0, m + 1, eight_shifts, sums)
        for t in range(8):
            nbr_x[8 * m + t] = jnp.broadcast_to(here[t:t + 1, :] - CENTRE, (16, A)).astype(BF16)
            for cj in range(9):
                h_x[cj, 8 * m + t] = jnp.broadcast_to(sums[cj][t:t + 1, :], (16, A)).astype(BF16)
        return 0

    lax.fori_loop(0, 8, eight_slots, 0)


def weight_rows(block, nbr_x, h_x):
    ids = (iota((16, A), 0) + (block * 32 - CENTRE)).astype(F32)
    low, high = ids.astype(BF16), (ids + 16.0).astype(BF16)
    zero = jnp.zeros((16, A), BF16)

    def many_slots(g, sums):
        for t in range(UNROLL):
            k = g * UNROLL + t
            row = nbr_x[k]
            at_low, at_high = row == low, row == high
            out = []
            for cj in range(9):
                value = h_x[cj, k]
                out.append(jnp.where(at_low, value, sums[2 * cj]))
                out.append(jnp.where(at_high, value, sums[2 * cj + 1]))
            sums = tuple(out)
        return sums

    return lax.fori_loop(0, K // UNROLL, many_slots, (zero,) * 18)


def kernel(
    n_wide, n_narrow, per_z, z_high,
    vec_in, hess_in, nbr_in, halo_in, lab_in, mass_in, rot_in,
    gram_ref, out_ref,
    vec_ref, hess_ref, nbr_ref, halo_ref, lab_ref, mass_ref, rot_ref,
    x_ref, nbr_pad, h_pad, nbr_x, h_x, w_local, w_halo, wt_halo, g_ref, first_ref, part_ref, second_ref, turned_ref,
    load_sem, halo_send, halo_recv, send_sem, recv_sem, relay_sem,
):
    p, q = lax.axis_index("wide"), lax.axis_index("narrow")
    z_low = n_wide // per_z
    n_x = n_narrow // z_high
    plane, along = per_z * n_x, z_low * z_high
    in_plane = lax.div(q, z_high) * per_z + lax.rem(p, per_z)
    in_z = lax.rem(q, z_high) * z_low + lax.div(p, per_z)

    n_y = per_z // 2
    x_at, y_at, core = lax.div(q, z_high), lax.div(lax.rem(p, per_z), 2), lax.rem(p, 2)
    p_plane, q_plane = p - lax.rem(p, per_z), lax.rem(q, z_high)
    p_z, q_z = lax.rem(p, per_z), q - lax.rem(q, z_high)
    xs = [lax.rem(x_at + d, n_x) for d in range(n_x)]
    ys = [lax.rem(y_at + d, n_y) * 2 for d in range(n_y)]
    cores = [core, 1 - core]
    tops = [q_plane + x * z_high for x in xs]
    lows = [[y + c for c in cores] for y in ys]

    def plane_device(d):
        dx, dy, dc = d // per_z, d // 2 % n_y, d % 2
        return (p_plane + lows[dy][dc], tops[dx]), xs[dx] * per_z + lows[dy][dc]

    def z_device(d):
        at = lax.rem(in_z + d, along)
        return lax.rem(at, z_low) * per_z + p_z, q_z + lax.div(at, z_low)

    def back(d):
        dx, dy, dc = d // per_z, d // 2 % n_y, d % 2
        return (-dx % n_x) * per_z + (-dy % n_y) * 2 + dc

    has = {"up": p > 0, "down": p < n_wide - 1, "left": q > 0, "right": q < n_narrow - 1}
    where = {"up": (p - 1, q), "down": (p + 1, q), "left": (p, q - 1), "right": (p, q + 1)}

    for name, index in (("left", 0), ("right", 2)):
        @pl.when(jnp.logical_not(has[name]))
        def _():
            x_ref[1, index] = jnp.zeros((PAY, V), BF16)
    for name, index in (("up", 0), ("down", 2)):
        @pl.when(jnp.logical_not(has[name]))
        def _():
            x_ref[index] = jnp.zeros((3, PAY, V), BF16)

    barrier = pltpu.get_barrier_semaphore()

    def greet(device):
        pl.semaphore_signal(barrier, inc=1, device_id=device, device_id_type=MESH)

    for name in has:
        @pl.when(has[name])
        def _():
            greet(where[name])

    reach = along // 4
    for d in range(reach, 0, -1):
        greet(z_device(d))
        greet(z_device(along - d))
    for d in range(1, plane):
        greet(plane_device(d)[0])

    loads = [
        pltpu.make_async_copy(source, target, load_sem.at[number])
        for number, (source, target) in enumerate((
            (halo_in, halo_ref), (lab_in, lab_ref), (mass_in, mass_ref), (vec_in, vec_ref),
            (nbr_in, nbr_ref), (hess_in, hess_ref), (rot_in, rot_ref),
        ))
    ]
    for load in loads:
        load.start()
    for load in loads[:4]:
        load.wait()

    masses = mass_ref[...]
    roots = lax.rsqrt(masses)
    roots = roots * (1.5 - 0.5 * masses * roots * roots)
    pick = lax.rem(iota((A, NISO), 0), NISO) == iota((A, NISO), 1)
    group = iota((A, V), 0)
    table = []
    for iso in range(2):
        column = jnp.sum(jnp.where(pick, roots[iso:iso + 1, :], 0.0), axis=1, keepdims=True)
        full = jnp.broadcast_to(column, (A, V))
        one = full.astype(BF16).astype(F32)
        two = (full - one).astype(BF16).astype(F32)
        three = full - one - two
        table.append(
            jnp.where(group < 16, one, jnp.where(group < 32, two, jnp.where(group < 48, three, 0.0))).astype(BF16)
        )
    table = jnp.concatenate(table, axis=1)
    table_two = jnp.concatenate([jnp.zeros((V // 2, 2 * V), BF16), table[:V // 2]], axis=0)
    half = lax.rem(group, V // 2)
    classes = jnp.where(
        (lax.rem(group, NISO) == lab_ref[...]) & (half < 3 * NISO), 1.0, 0.0
    ).T.astype(BF16)
    factors = dot(classes, table)

    boundary = jnp.where(iota((A, H), 0) == halo_ref[...], 1.0, 0.0).astype(BF16)
    for j in range(3):
        x_ref[1, 1, j * H:(j + 1) * H, :] = dot(boundary, vec_ref[j], ((0,), (0,))).astype(BF16)
    chosen = dot(boundary, classes, ((0,), (0,)))
    x_ref[1, 1, 3 * H:, :] = jnp.where(
        iota((H // 2, V), 1) < V // 2, chosen[:H // 2], chosen[H // 2:]
    ).astype(BF16)

    for load in loads[4:]:
        load.wait()
    vectors = [vec_ref[j] for j in range(3)]
    stacked = vec_ref[...].reshape(3 * A, V)
    turned = stacked.astype(F32).T.astype(BF16)

    combine_duplicates(nbr_ref, hess_ref, nbr_pad, h_pad, nbr_x, h_x)

    def local_block(block, _):
        rows = weight_rows(block, nbr_x, h_x)
        for cj in range(9):
            at = pl.multiple_of(block * 32, 32)
            w_local[cj, pl.ds(at, 16), :] = rows[2 * cj]
            w_local[cj, pl.ds(pl.multiple_of(at + 16, 16), 16), :] = rows[2 * cj + 1]
        return 0

    lax.fori_loop(0, 2, local_block, 0)

    greetings = plane - 1 + 2 * reach
    for name in has:
        greetings = greetings + has[name].astype(jnp.int32)
    pl.semaphore_wait(barrier, greetings)

    def halo_copy(j, at, name):
        number = at[0] * 3 + at[1]
        return pltpu.make_async_remote_copy(
            src_ref=x_ref.at[1, j], dst_ref=x_ref.at[at[0], at[1]],
            send_sem=halo_send.at[number], recv_sem=halo_recv.at[number],
            device_id=where[name], device_id_type=MESH,
        )

    to_right, to_left = halo_copy(1, (1, 0), "right"), halo_copy(1, (1, 2), "left")
    to_down = [halo_copy(j, (0, j), "down") for j in range(3)]
    to_up = [halo_copy(j, (2, j), "up") for j in range(3)]
    pl.when(has["right"])(to_right.start)
    pl.when(has["left"])(to_left.start)
    pl.when(has["down"])(to_down[1].start)
    pl.when(has["up"])(to_up[1].start)

    for d in (reach, along - reach):
        pl.semaphore_signal(relay_sem, inc=1, device_id=z_device(d), device_id_type=MESH)

    def halo_block(block, _):
        rows = weight_rows(block + A // 32, nbr_x, h_x)
        for cj in range(9):
            at = (cj % 3) * H
            w_halo[cj // 3, block, at:at + 16, :] = rows[2 * cj]
            w_halo[cj // 3, block, at + 16:at + 32, :] = rows[2 * cj + 1]
        return 0

    lax.fori_loop(2, A // 32, local_block, 0)
    lax.fori_loop(0, 9, halo_block, 0)

    own = iota((A, A), 0) == iota((A, A), 1)
    scaled = [
        (jnp.concatenate([v.astype(F32)] * 2, axis=1) * factors).astype(BF16) for v in vectors
    ]
    scaled = jnp.concatenate(scaled, axis=0)
    products = []
    for c in range(3):
        diagonal = jnp.concatenate(
            [jnp.where(own, hess_ref[c, j, 0:1, :].astype(F32), 0.0).astype(BF16) for j in range(3)], axis=1
        )
        near = jnp.concatenate([w_local[c * 3 + j].T for j in range(3)], axis=1)
        products.append(dot(diagonal, scaled) + dot(near, scaled))
        wt_halo[c * A:(c + 1) * A, :] = jnp.concatenate([w_halo[c, b] for b in CORNERS], axis=0).T

    def far_rows(blocks):
        out = []
        for b in blocks:
            block = x_ref[b // 3, b % 3]
            packed = block[3 * H:]
            scale = jnp.concatenate([dot(packed, table), dot(packed, table_two)], axis=0)
            for j in range(3):
                rows = block[j * H:(j + 1) * H].astype(F32)
                out.append((jnp.concatenate([rows, rows], axis=1) * scale).astype(BF16))
        return jnp.concatenate(out, axis=0)

    pl.when(has["left"])(to_right.wait_recv)
    pl.when(has["down"])(to_down[0].start)
    pl.when(has["up"])(to_up[0].start)
    pl.when(has["right"])(to_left.wait_recv)
    pl.when(has["down"])(to_down[2].start)
    pl.when(has["up"])(to_up[2].start)

    for name, copies in (("up", to_down), ("down", to_up)):
        pl.when(has[name])(copies[1].wait_recv)
    edge_rows = far_rows(EDGES)
    for c in range(3):
        edges = jnp.concatenate([w_halo[c, b] for b in EDGES], axis=0).T
        products[c] += dot(edges, edge_rows)
    early = jnp.concatenate(products, axis=0)
    all_factors = jnp.concatenate([factors] * 3, axis=0)

    for name, copies in (("up", to_down), ("down", to_up)):
        @pl.when(has[name])
        def _():
            copies[0].wait_recv()
            copies[2].wait_recv()

    product = early + dot(wt_halo[...], far_rows(CORNERS))
    image = product * all_factors
    image_high, image_low = split(image)
    gram = dot(turned, image_high) + dot(turned, image_low)
    rows = 2 * V // plane
    for iso in range(2):
        g_ref[iso * (plane // 2):(iso + 1) * (plane // 2)] = gram[:, iso * V:(iso + 1) * V].reshape(plane // 2, rows, V)

    def scatter(d):
        device, target = plane_device(d)
        pltpu.make_async_remote_copy(
            src_ref=g_ref.at[target], dst_ref=first_ref.at[back(d) - 1],
            send_sem=send_sem.at[0], recv_sem=recv_sem.at[0],
            device_id=device, device_id_type=MESH,
        ).start()

    def ring(distance, size):
        return min(distance % size, -distance % size)

    plane_order = sorted(
        range(1, plane), key=lambda d: -ring(d // per_z, n_x) - ring(d // 2 % n_y, n_y)
    )
    z_order = sorted(range(1, along), key=lambda d: -ring(d, along))
    for d in plane_order:
        scatter(d)

    def arrived(ref, number):
        pltpu.make_async_copy(ref, ref, recv_sem.at[number]).wait()

    def sent(ref, number):
        pltpu.make_async_copy(ref, ref, send_sem.at[number]).wait()

    rotations = [split(rot_ref[iso]) for iso in range(2)]
    for iso in range(2):
        high, low = image_high[:, iso * V:(iso + 1) * V], image_low[:, iso * V:(iso + 1) * V]
        r_high, r_low = rotations[iso]
        turned_ref[iso] = dot(high, r_high) + (dot(high, r_low) + dot(low, r_high))

    arrived(first_ref, 0)
    part_ref[0] = g_ref[in_plane] + jnp.sum(first_ref[...], axis=0)

    def exchange(d):
        pltpu.make_async_remote_copy(
            src_ref=part_ref.at[0], dst_ref=second_ref.at[along - 1 - d],
            send_sem=send_sem.at[1], recv_sem=recv_sem.at[1],
            device_id=z_device(d), device_id_type=MESH,
        ).start()

    pl.semaphore_wait(relay_sem, 2)
    for d in z_order:
        exchange(d)
    arrived(second_ref, 1)
    atoms_all = 3.0 * A * n_wide * n_narrow
    total = (part_ref[0] + jnp.sum(second_ref[...], axis=0)) / atoms_all
    sent(first_ref, 0)
    final_ref = part_ref.at[1]
    final_ref[...] = total

    def gather(d):
        device, _ = plane_device(d)
        pltpu.make_async_remote_copy(
            src_ref=final_ref, dst_ref=gram_ref.at[in_plane],
            send_sem=send_sem.at[2], recv_sem=recv_sem.at[2],
            device_id=device, device_id_type=MESH,
        ).start()

    for d in plane_order:
        gather(d)
    gram_ref[in_plane] = total
    arrived(first_ref, 2)
    for iso in range(2):
        whole = gram_ref[iso * (plane // 2):(iso + 1) * (plane // 2)].reshape(V, V)
        high, low = split(whole)
        r_high, r_low = rotations[iso]
        m_high, m_low = split(dot(high, r_high) + (dot(high, r_low) + dot(low, r_high)))
        out_ref[iso] = (
            turned_ref[iso] - (dot(stacked, m_high) + dot(stacked, m_low))
        ).astype(BF16).reshape(3, A, V)

    sent(second_ref, 1)
    sent(first_ref, 2)
    pl.when(has["right"])(to_right.wait_send)
    pl.when(has["left"])(to_left.wait_send)
    for name, copies in (("down", to_down), ("up", to_up)):
        @pl.when(has[name])
        def _():
            for copy in copies:
                copy.wait_send()


def local(n_wide, n_narrow, per_z, z_high, vectors, hessian, neighbours, halo_atoms, labels, masses, rotation):
    plane = per_z * (n_narrow // z_high)
    along = (n_wide // per_z) * z_high
    rows = 2 * V // plane
    vmem = pl.BlockSpec(memory_space=pltpu.VMEM)
    gram, rotated = pl.pallas_call(
        functools.partial(kernel, n_wide, n_narrow, per_z, z_high),
        out_shape=(
            pltpu.VMEM((plane, rows, V), F32),
            pltpu.VMEM((2, 3, A, V), BF16),
        ),
        in_specs=[pl.BlockSpec(memory_space=pltpu.HBM)] * 7,
        out_specs=(vmem, vmem),
        scratch_shapes=[
            pltpu.VMEM((3, A, V), BF16),
            pltpu.VMEM((3, 3, 1 + K, A), BF16),
            pltpu.VMEM((K, A), jnp.int32),
            pltpu.VMEM((1, H), jnp.int32),
            pltpu.VMEM((1, A), jnp.int32),
            pltpu.VMEM((2, NISO), F32),
            pltpu.VMEM((2, V, V), F32),
            pltpu.VMEM((3, 3, PAY, V), BF16),
            pltpu.VMEM((128, A), F32),
            pltpu.VMEM((9, 128, A), F32),
            pltpu.VMEM((64, 16, A), BF16),
            pltpu.VMEM((9, 64, 16, A), BF16),
            pltpu.VMEM((9, A, A), BF16),
            pltpu.VMEM((3, 9, 3 * H, A), BF16),
            pltpu.VMEM((3 * A, 12 * H), BF16),
            pltpu.VMEM((plane, rows, V), F32),
            pltpu.VMEM((plane - 1, rows, V), F32),
            pltpu.VMEM((2, rows, V), F32),
            pltpu.VMEM((along - 1, rows, V), F32),
            pltpu.VMEM((2, 3 * A, V), F32),
            pltpu.SemaphoreType.DMA((7,)),
            pltpu.SemaphoreType.DMA((9,)),
            pltpu.SemaphoreType.DMA((9,)),
            pltpu.SemaphoreType.DMA((3,)),
            pltpu.SemaphoreType.DMA((3,)),
            pltpu.SemaphoreType.REGULAR,
        ],
        compiler_params=pltpu.CompilerParams(
            collective_id=0, has_side_effects=True, vmem_limit_bytes=60 * 1024 * 1024
        ),
    )(vectors, hessian, neighbours, halo_atoms.reshape(1, H), labels.reshape(1, A), masses, rotation)
    return gram.reshape(2, V, V), rotated


def solution(mesh):
    n_wide, n_narrow = mesh.shape["wide"], mesh.shape["narrow"]
    per_z = n_wide // 4 if n_wide >= 16 else n_wide // 2
    z_high = 4 if n_narrow >= 16 else n_narrow // 2
    spread = ("wide", "narrow")
    return jax.shard_map(
        functools.partial(local, n_wide, n_narrow, per_z, z_high),
        mesh=mesh,
        in_specs=(
            P(None, spread, None),
            P(None, None, None, spread),
            P(None, spread),
            P(spread),
            P(spread),
            P(),
            P(),
        ),
        out_specs=(P(), P(None, None, spread, None)),
        check_vma=False,
    )
```

```python
import functools

import jax
import jax.numpy as jnp
from jax import lax
from jax.experimental import pallas as pl
from jax.experimental.pallas import tpu as pltpu
from jax.sharding import PartitionSpec as P

MESH = pl.DeviceIdType.MESH
F32 = jnp.float32
BF16 = jnp.bfloat16
A = 128
H = 32
V = 128
K = 60
UNROLL = 30
ROWS = A + 9 * H
NISO = 16
CORNERS, EDGES = (0, 2, 6, 8), (1, 3, 4, 5, 7)
PAY = 3 * H + H // 2
CENTRE = ROWS // 2


def dot(x, y, dims=((1,), (0,))):
    return lax.dot_general(x, y, (dims, ((), ())), preferred_element_type=F32)


def split(x):
    high = x.astype(BF16)
    return high, (x - high.astype(F32)).astype(BF16)


def iota(shape, dim):
    return lax.broadcasted_iota(jnp.int32, shape, dim)


def combine_duplicates(nbr_ref, hess_ref, nbr_pad, h_pad, nbr_x, h_x):
    nbr_pad[0:64, :] = jnp.full((64, A), -1.0, F32)
    nbr_pad[64:64 + K, :] = nbr_ref[...].astype(F32)
    nbr_pad[64 + K:128, :] = jnp.full((64 - K, A), -2.0, F32)
    for cj in range(9):
        h_pad[cj, 0:64, :] = jnp.zeros((64, A), F32)
        h_pad[cj, 64:64 + K, :] = hess_ref[cj // 3, cj % 3, 1:1 + K, :].astype(F32)
        h_pad[cj, 64 + K:128, :] = jnp.zeros((64 - K, A), F32)

    def eight_slots(m, _):
        first = 64 + 8 * m
        here = nbr_pad[pl.ds(first, 8), :]
        sums = tuple(h_pad[cj, pl.ds(first, 8), :] for cj in range(9))

        def eight_shifts(g, sums):
            for t in range(8):
                back = first - (8 * g + t + 1)
                same = nbr_pad[pl.ds(back, 8), :] == here
                sums = tuple(
                    s + jnp.where(same, h_pad[cj, pl.ds(back, 8), :], 0.0) for cj, s in enumerate(sums)
                )
            return sums

        sums = lax.fori_loop(0, m + 1, eight_shifts, sums)
        for t in range(8):
            nbr_x[8 * m + t] = jnp.broadcast_to(here[t:t + 1, :] - CENTRE, (16, A)).astype(BF16)
            for cj in range(9):
                h_x[cj, 8 * m + t] = jnp.broadcast_to(sums[cj][t:t + 1, :], (16, A)).astype(BF16)
        return 0

    lax.fori_loop(0, 8, eight_slots, 0)


def weight_rows(block, nbr_x, h_x):
    ids = (iota((16, A), 0) + (block * 32 - CENTRE)).astype(F32)
    low, high = ids.astype(BF16), (ids + 16.0).astype(BF16)
    zero = jnp.zeros((16, A), BF16)

    def many_slots(g, sums):
        for t in range(UNROLL):
            k = g * UNROLL + t
            row = nbr_x[k]
            at_low, at_high = row == low, row == high
            out = []
            for cj in range(9):
                value = h_x[cj, k]
                out.append(jnp.where(at_low, value, sums[2 * cj]))
                out.append(jnp.where(at_high, value, sums[2 * cj + 1]))
            sums = tuple(out)
        return sums

    return lax.fori_loop(0, K // UNROLL, many_slots, (zero,) * 18)


def kernel(
    n_wide, n_narrow, per_z, z_high,
    vec_in, hess_in, nbr_in, halo_in, lab_in, mass_in, rot_in,
    gram_ref, turned_ref,
    vec_ref, hess_ref, nbr_ref, halo_ref, lab_ref, mass_ref, rot_ref,
    x_ref, nbr_pad, h_pad, nbr_x, h_x, w_local, w_halo, wt_halo, g_ref, first_ref, part_ref, second_ref,
    load_sem, halo_send, halo_recv, send_sem, recv_sem, relay_sem,
):
    p, q = lax.axis_index("wide"), lax.axis_index("narrow")
    z_low = n_wide // per_z
    n_x = n_narrow // z_high
    plane, along = per_z * n_x, z_low * z_high
    in_plane = lax.div(q, z_high) * per_z + lax.rem(p, per_z)
    in_z = lax.rem(q, z_high) * z_low + lax.div(p, per_z)

    n_y = per_z // 2
    x_at, y_at, core = lax.div(q, z_high), lax.div(lax.rem(p, per_z), 2), lax.rem(p, 2)
    p_plane, q_plane = p - lax.rem(p, per_z), lax.rem(q, z_high)
    p_z, q_z = lax.rem(p, per_z), q - lax.rem(q, z_high)
    xs = [lax.rem(x_at + d, n_x) for d in range(n_x)]
    ys = [lax.rem(y_at + d, n_y) * 2 for d in range(n_y)]
    cores = [core, 1 - core]
    tops = [q_plane + x * z_high for x in xs]
    lows = [[y + c for c in cores] for y in ys]

    def plane_device(d):
        dx, dy, dc = d // per_z, d // 2 % n_y, d % 2
        return (p_plane + lows[dy][dc], tops[dx]), xs[dx] * per_z + lows[dy][dc]

    def z_device(d):
        at = lax.rem(in_z + d, along)
        return lax.rem(at, z_low) * per_z + p_z, q_z + lax.div(at, z_low)

    def back(d):
        dx, dy, dc = d // per_z, d // 2 % n_y, d % 2
        return (-dx % n_x) * per_z + (-dy % n_y) * 2 + dc

    has = {"up": p > 0, "down": p < n_wide - 1, "left": q > 0, "right": q < n_narrow - 1}
    where = {"up": (p - 1, q), "down": (p + 1, q), "left": (p, q - 1), "right": (p, q + 1)}

    for name, index in (("left", 0), ("right", 2)):
        @pl.when(jnp.logical_not(has[name]))
        def _():
            x_ref[1, index] = jnp.zeros((PAY, V), BF16)
    for name, index in (("up", 0), ("down", 2)):
        @pl.when(jnp.logical_not(has[name]))
        def _():
            x_ref[index] = jnp.zeros((3, PAY, V), BF16)

    barrier = pltpu.get_barrier_semaphore()

    def greet(device):
        pl.semaphore_signal(barrier, inc=1, device_id=device, device_id_type=MESH)

    for name in has:
        @pl.when(has[name])
        def _():
            greet(where[name])

    reach = along // 4
    for d in range(reach, 0, -1):
        greet(z_device(d))
        greet(z_device(along - d))
    for d in range(1, plane):
        greet(plane_device(d)[0])

    loads = [
        pltpu.make_async_copy(source, target, load_sem.at[number])
        for number, (source, target) in enumerate((
            (halo_in, halo_ref), (lab_in, lab_ref), (mass_in, mass_ref), (vec_in, vec_ref),
            (nbr_in, nbr_ref), (hess_in, hess_ref), (rot_in, rot_ref),
        ))
    ]
    for load in loads:
        load.start()
    for load in loads[:4]:
        load.wait()

    masses = mass_ref[...]
    roots = lax.rsqrt(masses)
    roots = roots * (1.5 - 0.5 * masses * roots * roots)
    pick = lax.rem(iota((A, NISO), 0), NISO) == iota((A, NISO), 1)
    group = iota((A, V), 0)
    table = []
    for iso in range(2):
        column = jnp.sum(jnp.where(pick, roots[iso:iso + 1, :], 0.0), axis=1, keepdims=True)
        full = jnp.broadcast_to(column, (A, V))
        one = full.astype(BF16).astype(F32)
        two = (full - one).astype(BF16).astype(F32)
        three = full - one - two
        table.append(
            jnp.where(group < 16, one, jnp.where(group < 32, two, jnp.where(group < 48, three, 0.0))).astype(BF16)
        )
    table = jnp.concatenate(table, axis=1)
    table_two = jnp.concatenate([jnp.zeros((V // 2, 2 * V), BF16), table[:V // 2]], axis=0)
    half = lax.rem(group, V // 2)
    classes = jnp.where(
        (lax.rem(group, NISO) == lab_ref[...]) & (half < 3 * NISO), 1.0, 0.0
    ).T.astype(BF16)
    factors = dot(classes, table)

    boundary = jnp.where(iota((A, H), 0) == halo_ref[...], 1.0, 0.0).astype(BF16)
    for j in range(3):
        x_ref[1, 1, j * H:(j + 1) * H, :] = dot(boundary, vec_ref[j], ((0,), (0,))).astype(BF16)
    chosen = dot(boundary, classes, ((0,), (0,)))
    x_ref[1, 1, 3 * H:, :] = jnp.where(
        iota((H // 2, V), 1) < V // 2, chosen[:H // 2], chosen[H // 2:]
    ).astype(BF16)

    for load in loads[4:]:
        load.wait()
    vectors = [vec_ref[j] for j in range(3)]
    stacked = vec_ref[...].reshape(3 * A, V)
    turned = stacked.astype(F32).T.astype(BF16)

    combine_duplicates(nbr_ref, hess_ref, nbr_pad, h_pad, nbr_x, h_x)

    def local_block(block, _):
        rows = weight_rows(block, nbr_x, h_x)
        for cj in range(9):
            at = pl.multiple_of(block * 32, 32)
            w_local[cj, pl.ds(at, 16), :] = rows[2 * cj]
            w_local[cj, pl.ds(pl.multiple_of(at + 16, 16), 16), :] = rows[2 * cj + 1]
        return 0

    lax.fori_loop(0, 2, local_block, 0)

    greetings = plane - 1 + 2 * reach
    for name in has:
        greetings = greetings + has[name].astype(jnp.int32)
    pl.semaphore_wait(barrier, greetings)

    def halo_copy(j, at, name):
        number = at[0] * 3 + at[1]
        return pltpu.make_async_remote_copy(
            src_ref=x_ref.at[1, j], dst_ref=x_ref.at[at[0], at[1]],
            send_sem=halo_send.at[number], recv_sem=halo_recv.at[number],
            device_id=where[name], device_id_type=MESH,
        )

    to_right, to_left = halo_copy(1, (1, 0), "right"), halo_copy(1, (1, 2), "left")
    to_down = [halo_copy(j, (0, j), "down") for j in range(3)]
    to_up = [halo_copy(j, (2, j), "up") for j in range(3)]
    pl.when(has["right"])(to_right.start)
    pl.when(has["left"])(to_left.start)
    pl.when(has["down"])(to_down[1].start)
    pl.when(has["up"])(to_up[1].start)

    for d in (reach, along - reach):
        pl.semaphore_signal(relay_sem, inc=1, device_id=z_device(d), device_id_type=MESH)

    def halo_block(block, _):
        rows = weight_rows(block + A // 32, nbr_x, h_x)
        for cj in range(9):
            at = (cj % 3) * H
            w_halo[cj // 3, block, at:at + 16, :] = rows[2 * cj]
            w_halo[cj // 3, block, at + 16:at + 32, :] = rows[2 * cj + 1]
        return 0

    lax.fori_loop(2, A // 32, local_block, 0)
    lax.fori_loop(0, 9, halo_block, 0)

    pl.when(has["left"])(to_right.wait_recv)
    pl.when(has["down"])(to_down[0].start)
    pl.when(has["up"])(to_up[0].start)
    pl.when(has["right"])(to_left.wait_recv)
    pl.when(has["down"])(to_down[2].start)
    pl.when(has["up"])(to_up[2].start)

    own = iota((A, A), 0) == iota((A, A), 1)
    scaled = [
        (jnp.concatenate([v.astype(F32)] * 2, axis=1) * factors).astype(BF16) for v in vectors
    ]
    scaled = jnp.concatenate(scaled, axis=0)
    products = []
    for c in range(3):
        diagonal = jnp.concatenate(
            [jnp.where(own, hess_ref[c, j, 0:1, :].astype(F32), 0.0).astype(BF16) for j in range(3)], axis=1
        )
        near = jnp.concatenate([w_local[c * 3 + j].T for j in range(3)], axis=1)
        products.append(dot(diagonal, scaled) + dot(near, scaled))
        wt_halo[c * A:(c + 1) * A, :] = jnp.concatenate([w_halo[c, b] for b in CORNERS], axis=0).T

    def far_rows(blocks):
        out = []
        for b in blocks:
            block = x_ref[b // 3, b % 3]
            packed = block[3 * H:]
            scale = jnp.concatenate([dot(packed, table), dot(packed, table_two)], axis=0)
            for j in range(3):
                rows = block[j * H:(j + 1) * H].astype(F32)
                out.append((jnp.concatenate([rows, rows], axis=1) * scale).astype(BF16))
        return jnp.concatenate(out, axis=0)

    for name, copies in (("up", to_down), ("down", to_up)):
        pl.when(has[name])(copies[1].wait_recv)
    edge_rows = far_rows(EDGES)
    for c in range(3):
        edges = jnp.concatenate([w_halo[c, b] for b in EDGES], axis=0).T
        products[c] += dot(edges, edge_rows)
    early = jnp.concatenate(products, axis=0)
    all_factors = jnp.concatenate([factors] * 3, axis=0)
    first_high, first_low = split(early * all_factors)
    first_gram = dot(turned, first_high) + dot(turned, first_low)
    corner_weights = wt_halo[...]
    corner_left = []
    for iso in range(2):
        scale = jnp.concatenate([all_factors[:, iso * V:(iso + 1) * V]] * 3, axis=1)
        high, low = split(corner_weights.astype(F32) * scale)
        corner_left.append(split(dot(turned, high) + dot(turned, low)))

    for name, copies in (("up", to_down), ("down", to_up)):
        @pl.when(has[name])
        def _():
            copies[0].wait_recv()
            copies[2].wait_recv()

    corner_rows = far_rows(CORNERS)
    rows = 2 * V // plane
    for iso in range(2):
        high, low = corner_left[iso]
        right = corner_rows[:, iso * V:(iso + 1) * V]
        gram = first_gram[:, iso * V:(iso + 1) * V] + (dot(high, right) + dot(low, right))
        g_ref[iso * (plane // 2):(iso + 1) * (plane // 2)] = gram.reshape(plane // 2, rows, V)

    def scatter(d):
        device, target = plane_device(d)
        pltpu.make_async_remote_copy(
            src_ref=g_ref.at[target], dst_ref=first_ref.at[back(d) - 1],
            send_sem=send_sem.at[0], recv_sem=recv_sem.at[0],
            device_id=device, device_id_type=MESH,
        ).start()

    def ring(distance, size):
        return min(distance % size, -distance % size)

    plane_order = sorted(
        range(1, plane), key=lambda d: -ring(d // per_z, n_x) - ring(d // 2 % n_y, n_y)
    )
    z_order = sorted(range(1, along), key=lambda d: -ring(d, along))
    for d in plane_order:
        scatter(d)

    def arrived(ref, number):
        pltpu.make_async_copy(ref, ref, recv_sem.at[number]).wait()

    def sent(ref, number):
        pltpu.make_async_copy(ref, ref, send_sem.at[number]).wait()

    product = early + dot(corner_weights, corner_rows)
    image_high, image_low = split(product * all_factors)
    rotations = [split(rot_ref[iso]) for iso in range(2)]
    for iso in range(2):
        high, low = image_high[:, iso * V:(iso + 1) * V], image_low[:, iso * V:(iso + 1) * V]
        r_high, r_low = rotations[iso]
        turned_ref[iso] = dot(high, r_high) + (dot(high, r_low) + dot(low, r_high))

    arrived(first_ref, 0)
    part_ref[0] = g_ref[in_plane] + jnp.sum(first_ref[...], axis=0)

    def exchange(d):
        pltpu.make_async_remote_copy(
            src_ref=part_ref.at[0], dst_ref=second_ref.at[along - 1 - d],
            send_sem=send_sem.at[1], recv_sem=recv_sem.at[1],
            device_id=z_device(d), device_id_type=MESH,
        ).start()

    pl.semaphore_wait(relay_sem, 2)
    for d in z_order:
        exchange(d)
    arrived(second_ref, 1)
    atoms_all = 3.0 * A * n_wide * n_narrow
    total = (part_ref[0] + jnp.sum(second_ref[...], axis=0)) / atoms_all
    sent(first_ref, 0)
    final_ref = part_ref.at[1]
    final_ref[...] = total

    def gather(d):
        device, _ = plane_device(d)
        pltpu.make_async_remote_copy(
            src_ref=final_ref, dst_ref=gram_ref.at[in_plane],
            send_sem=send_sem.at[2], recv_sem=recv_sem.at[2],
            device_id=device, device_id_type=MESH,
        ).start()

    for d in plane_order:
        gather(d)
    gram_ref[in_plane] = total
    arrived(first_ref, 2)
    sent(second_ref, 1)
    sent(first_ref, 2)
    pl.when(has["right"])(to_right.wait_send)
    pl.when(has["left"])(to_left.wait_send)
    for name, copies in (("down", to_down), ("up", to_up)):
        @pl.when(has[name])
        def _():
            for copy in copies:
                copy.wait_send()


def finish(gram_ref, turned_ref, vec_in, rot_in, gram_out, out_ref, vec_ref, rot_ref, rotated_ref, sem):
    loads = [
        pltpu.make_async_copy(vec_in, vec_ref, sem.at[0]),
        pltpu.make_async_copy(rot_in, rot_ref, sem.at[1]),
    ]
    stores = [pltpu.make_async_copy(gram_ref, gram_out, sem.at[2])]
    for copy in loads + stores:
        copy.start()
    for load in loads:
        load.wait()
    half = gram_ref.shape[0] // 2
    stacked = vec_ref[...].reshape(3 * A, V)
    for iso in range(2):
        high, low = split(gram_ref[iso * half:(iso + 1) * half].reshape(V, V))
        r_high, r_low = split(rot_ref[iso])
        m_high, m_low = split(dot(high, r_high) + (dot(high, r_low) + dot(low, r_high)))
        rotated_ref[iso] = (
            turned_ref[iso] - (dot(stacked, m_high) + dot(stacked, m_low))
        ).astype(BF16).reshape(3, A, V)
        stores.append(pltpu.make_async_copy(rotated_ref.at[iso], out_ref.at[iso], sem.at[3 + iso]))
        stores[-1].start()
    for store in stores:
        store.wait()


def local(n_wide, n_narrow, per_z, z_high, vectors, hessian, neighbours, halo_atoms, labels, masses, rotation):
    plane = per_z * (n_narrow // z_high)
    along = (n_wide // per_z) * z_high
    rows = 2 * V // plane
    vmem = pl.BlockSpec(memory_space=pltpu.VMEM)
    gram, turned = pl.pallas_call(
        functools.partial(kernel, n_wide, n_narrow, per_z, z_high),
        out_shape=(
            pltpu.VMEM((plane, rows, V), F32),
            pltpu.VMEM((2, 3 * A, V), F32),
        ),
        in_specs=[pl.BlockSpec(memory_space=pltpu.HBM)] * 7,
        out_specs=(vmem, vmem),
        scratch_shapes=[
            pltpu.VMEM((3, A, V), BF16),
            pltpu.VMEM((3, 3, 1 + K, A), BF16),
            pltpu.VMEM((K, A), jnp.int32),
            pltpu.VMEM((1, H), jnp.int32),
            pltpu.VMEM((1, A), jnp.int32),
            pltpu.VMEM((2, NISO), F32),
            pltpu.VMEM((2, V, V), F32),
            pltpu.VMEM((3, 3, PAY, V), BF16),
            pltpu.VMEM((128, A), F32),
            pltpu.VMEM((9, 128, A), F32),
            pltpu.VMEM((64, 16, A), BF16),
            pltpu.VMEM((9, 64, 16, A), BF16),
            pltpu.VMEM((9, A, A), BF16),
            pltpu.VMEM((3, 9, 3 * H, A), BF16),
            pltpu.VMEM((3 * A, 12 * H), BF16),
            pltpu.VMEM((plane, rows, V), F32),
            pltpu.VMEM((plane - 1, rows, V), F32),
            pltpu.VMEM((2, rows, V), F32),
            pltpu.VMEM((along - 1, rows, V), F32),
            pltpu.SemaphoreType.DMA((7,)),
            pltpu.SemaphoreType.DMA((9,)),
            pltpu.SemaphoreType.DMA((9,)),
            pltpu.SemaphoreType.DMA((3,)),
            pltpu.SemaphoreType.DMA((3,)),
            pltpu.SemaphoreType.REGULAR,
        ],
        compiler_params=pltpu.CompilerParams(
            collective_id=0, has_side_effects=True, vmem_limit_bytes=60 * 1024 * 1024
        ),
    )(vectors, hessian, neighbours, halo_atoms.reshape(1, H), labels.reshape(1, A), masses, rotation)
    anywhere = pl.BlockSpec(memory_space=pl.ANY)
    gram, rotated = pl.pallas_call(
        finish,
        out_shape=(
            jax.ShapeDtypeStruct((plane, rows, V), F32),
            jax.ShapeDtypeStruct((2, 3, A, V), BF16),
        ),
        in_specs=[vmem, vmem, anywhere, anywhere],
        out_specs=(anywhere, anywhere),
        scratch_shapes=[
            pltpu.VMEM((3, A, V), BF16),
            pltpu.VMEM((2, V, V), F32),
            pltpu.VMEM((2, 3, A, V), BF16),
            pltpu.SemaphoreType.DMA((5,)),
        ],
        compiler_params=pltpu.CompilerParams(vmem_limit_bytes=8 * 1024 * 1024),
    )(gram, turned, vectors, rotation)
    return gram.reshape(2, V, V), rotated


def solution(mesh):
    n_wide, n_narrow = mesh.shape["wide"], mesh.shape["narrow"]
    per_z = n_wide // 4 if n_wide >= 16 else n_wide // 2
    z_high = 4 if n_narrow >= 16 else n_narrow // 2
    spread = ("wide", "narrow")
    return jax.shard_map(
        functools.partial(local, n_wide, n_narrow, per_z, z_high),
        mesh=mesh,
        in_specs=(
            P(None, spread, None),
            P(None, None, None, spread),
            P(None, spread),
            P(spread),
            P(spread),
            P(),
            P(),
        ),
        out_specs=(P(), P(None, None, spread, None)),
        check_vma=False,
    )
```

```python
import functools

import jax
import jax.numpy as jnp
from jax import lax
from jax.experimental import pallas as pl
from jax.experimental.pallas import tpu as pltpu
from jax.sharding import PartitionSpec as P

MESH = pl.DeviceIdType.MESH
F32 = jnp.float32
BF16 = jnp.bfloat16
A = 128
H = 32
V = 128
K = 60
UNROLL = 30
ROWS = A + 9 * H
NISO = 16
CORNERS, EDGES = (0, 2, 6, 8), (1, 3, 4, 5, 7)
PAY = 3 * H + H // 2
CENTRE = ROWS // 2


def dot(x, y, dims=((1,), (0,))):
    return lax.dot_general(x, y, (dims, ((), ())), preferred_element_type=F32)


def split(x):
    high = x.astype(BF16)
    return high, (x - high.astype(F32)).astype(BF16)


def iota(shape, dim):
    return lax.broadcasted_iota(jnp.int32, shape, dim)


def combine_duplicates(nbr_ref, hess_ref, nbr_pad, h_pad, nbr_x, h_x):
    nbr_pad[0:64, :] = jnp.full((64, A), -1.0, F32)
    nbr_pad[64:64 + K, :] = nbr_ref[...].astype(F32)
    nbr_pad[64 + K:128, :] = jnp.full((64 - K, A), -2.0, F32)
    for cj in range(9):
        h_pad[cj, 0:64, :] = jnp.zeros((64, A), F32)
        h_pad[cj, 64:64 + K, :] = hess_ref[cj // 3, cj % 3, 1:1 + K, :].astype(F32)
        h_pad[cj, 64 + K:128, :] = jnp.zeros((64 - K, A), F32)

    def eight_slots(m, _):
        first = 64 + 8 * m
        here = nbr_pad[pl.ds(first, 8), :]
        sums = tuple(h_pad[cj, pl.ds(first, 8), :] for cj in range(9))

        def eight_shifts(g, sums):
            for t in range(8):
                back = first - (8 * g + t + 1)
                same = nbr_pad[pl.ds(back, 8), :] == here
                sums = tuple(
                    s + jnp.where(same, h_pad[cj, pl.ds(back, 8), :], 0.0) for cj, s in enumerate(sums)
                )
            return sums

        sums = lax.fori_loop(0, m + 1, eight_shifts, sums)
        for t in range(8):
            nbr_x[8 * m + t] = jnp.broadcast_to(here[t:t + 1, :] - CENTRE, (16, A)).astype(BF16)
            for cj in range(9):
                h_x[cj, 8 * m + t] = jnp.broadcast_to(sums[cj][t:t + 1, :], (16, A)).astype(BF16)
        return 0

    lax.fori_loop(0, 8, eight_slots, 0)


def weight_rows(block, nbr_x, h_x):
    ids = (iota((16, A), 0) + (block * 32 - CENTRE)).astype(F32)
    low, high = ids.astype(BF16), (ids + 16.0).astype(BF16)
    zero = jnp.zeros((16, A), BF16)

    def many_slots(g, sums):
        for t in range(UNROLL):
            k = g * UNROLL + t
            row = nbr_x[k]
            at_low, at_high = row == low, row == high
            out = []
            for cj in range(9):
                value = h_x[cj, k]
                out.append(jnp.where(at_low, value, sums[2 * cj]))
                out.append(jnp.where(at_high, value, sums[2 * cj + 1]))
            sums = tuple(out)
        return sums

    return lax.fori_loop(0, K // UNROLL, many_slots, (zero,) * 18)


def kernel(
    n_wide, n_narrow, per_z, z_high,
    vec_in, hess_in, nbr_in, halo_in, lab_in, mass_in, rot_in,
    gram_ref, turned_ref,
    vec_ref, hess_ref, nbr_ref, halo_ref, lab_ref, mass_ref, rot_ref,
    x_ref, nbr_pad, h_pad, nbr_x, h_x, w_local, w_halo, wt_halo, g_ref, first_ref, part_ref, second_ref,
    load_sem, halo_send, halo_recv, send_sem, recv_sem, relay_sem,
):
    p, q = lax.axis_index("wide"), lax.axis_index("narrow")
    z_low = n_wide // per_z
    n_x = n_narrow // z_high
    plane, along = per_z * n_x, z_low * z_high
    in_plane = lax.div(q, z_high) * per_z + lax.rem(p, per_z)
    in_z = lax.rem(q, z_high) * z_low + lax.div(p, per_z)

    n_y = per_z // 2
    x_at, y_at, core = lax.div(q, z_high), lax.div(lax.rem(p, per_z), 2), lax.rem(p, 2)
    p_plane, q_plane = p - lax.rem(p, per_z), lax.rem(q, z_high)
    p_z, q_z = lax.rem(p, per_z), q - lax.rem(q, z_high)
    xs = [lax.rem(x_at + d, n_x) for d in range(n_x)]
    ys = [lax.rem(y_at + d, n_y) * 2 for d in range(n_y)]
    cores = [core, 1 - core]
    tops = [q_plane + x * z_high for x in xs]
    lows = [[y + c for c in cores] for y in ys]

    def plane_device(d):
        dx, dy, dc = d // per_z, d // 2 % n_y, d % 2
        return (p_plane + lows[dy][dc], tops[dx]), xs[dx] * per_z + lows[dy][dc]

    def z_device(d):
        at = lax.rem(in_z + d, along)
        return lax.rem(at, z_low) * per_z + p_z, q_z + lax.div(at, z_low)

    def back(d):
        dx, dy, dc = d // per_z, d // 2 % n_y, d % 2
        return (-dx % n_x) * per_z + (-dy % n_y) * 2 + dc

    has = {"up": p > 0, "down": p < n_wide - 1, "left": q > 0, "right": q < n_narrow - 1}
    where = {"up": (p - 1, q), "down": (p + 1, q), "left": (p, q - 1), "right": (p, q + 1)}

    for name, index in (("left", 0), ("right", 2)):
        @pl.when(jnp.logical_not(has[name]))
        def _():
            x_ref[1, index] = jnp.zeros((PAY, V), BF16)
    for name, index in (("up", 0), ("down", 2)):
        @pl.when(jnp.logical_not(has[name]))
        def _():
            x_ref[index] = jnp.zeros((3, PAY, V), BF16)

    barrier = pltpu.get_barrier_semaphore()

    def greet(device):
        pl.semaphore_signal(barrier, inc=1, device_id=device, device_id_type=MESH)

    for name in has:
        @pl.when(has[name])
        def _():
            greet(where[name])

    reach = along // 4
    for d in range(reach, 0, -1):
        greet(z_device(d))
        greet(z_device(along - d))
    for d in range(1, plane):
        greet(plane_device(d)[0])

    loads = [
        pltpu.make_async_copy(source, target, load_sem.at[number])
        for number, (source, target) in enumerate((
            (halo_in, halo_ref), (lab_in, lab_ref), (mass_in, mass_ref), (vec_in, vec_ref),
            (nbr_in, nbr_ref), (hess_in, hess_ref), (rot_in, rot_ref),
        ))
    ]
    for load in loads:
        load.start()
    for load in loads[:4]:
        load.wait()

    masses = mass_ref[...]
    roots = lax.rsqrt(masses)
    roots = roots * (1.5 - 0.5 * masses * roots * roots)
    pick = lax.rem(iota((A, NISO), 0), NISO) == iota((A, NISO), 1)
    group = iota((A, V), 0)
    table = []
    for iso in range(2):
        column = jnp.sum(jnp.where(pick, roots[iso:iso + 1, :], 0.0), axis=1, keepdims=True)
        full = jnp.broadcast_to(column, (A, V))
        one = full.astype(BF16).astype(F32)
        two = (full - one).astype(BF16).astype(F32)
        three = full - one - two
        table.append(
            jnp.where(group < 16, one, jnp.where(group < 32, two, jnp.where(group < 48, three, 0.0))).astype(BF16)
        )
    table = jnp.concatenate(table, axis=1)
    table_two = jnp.concatenate([jnp.zeros((V // 2, 2 * V), BF16), table[:V // 2]], axis=0)
    half = lax.rem(group, V // 2)
    classes = jnp.where(
        (lax.rem(group, NISO) == lab_ref[...]) & (half < 3 * NISO), 1.0, 0.0
    ).T.astype(BF16)
    factors = dot(classes, table)

    boundary = jnp.where(iota((A, H), 0) == halo_ref[...], 1.0, 0.0).astype(BF16)
    for j in range(3):
        x_ref[1, 1, j * H:(j + 1) * H, :] = dot(boundary, vec_ref[j], ((0,), (0,))).astype(BF16)
    chosen = dot(boundary, classes, ((0,), (0,)))
    x_ref[1, 1, 3 * H:, :] = jnp.where(
        iota((H // 2, V), 1) < V // 2, chosen[:H // 2], chosen[H // 2:]
    ).astype(BF16)

    for load in loads[4:]:
        load.wait()
    vectors = [vec_ref[j] for j in range(3)]
    stacked = vec_ref[...].reshape(3 * A, V)
    turned = stacked.astype(F32).T.astype(BF16)

    combine_duplicates(nbr_ref, hess_ref, nbr_pad, h_pad, nbr_x, h_x)

    def local_block(block, _):
        rows = weight_rows(block, nbr_x, h_x)
        for cj in range(9):
            at = pl.multiple_of(block * 32, 32)
            w_local[cj, pl.ds(at, 16), :] = rows[2 * cj]
            w_local[cj, pl.ds(pl.multiple_of(at + 16, 16), 16), :] = rows[2 * cj + 1]
        return 0

    lax.fori_loop(0, 2, local_block, 0)

    greetings = plane - 1 + 2 * reach
    for name in has:
        greetings = greetings + has[name].astype(jnp.int32)
    pl.semaphore_wait(barrier, greetings)

    def halo_copy(j, at, name):
        number = at[0] * 3 + at[1]
        return pltpu.make_async_remote_copy(
            src_ref=x_ref.at[1, j], dst_ref=x_ref.at[at[0], at[1]],
            send_sem=halo_send.at[number], recv_sem=halo_recv.at[number],
            device_id=where[name], device_id_type=MESH,
        )

    to_right, to_left = halo_copy(1, (1, 0), "right"), halo_copy(1, (1, 2), "left")
    to_down = [halo_copy(j, (0, j), "down") for j in range(3)]
    to_up = [halo_copy(j, (2, j), "up") for j in range(3)]
    pl.when(has["right"])(to_right.start)
    pl.when(has["left"])(to_left.start)
    pl.when(has["down"])(to_down[1].start)
    pl.when(has["up"])(to_up[1].start)

    for d in (reach, along - reach):
        pl.semaphore_signal(relay_sem, inc=1, device_id=z_device(d), device_id_type=MESH)

    def halo_block(block, _):
        rows = weight_rows(block + A // 32, nbr_x, h_x)
        for cj in range(9):
            at = (cj % 3) * H
            w_halo[cj // 3, block, at:at + 16, :] = rows[2 * cj]
            w_halo[cj // 3, block, at + 16:at + 32, :] = rows[2 * cj + 1]
        return 0

    lax.fori_loop(2, A // 32, local_block, 0)
    lax.fori_loop(0, 9, halo_block, 0)

    pl.when(has["left"])(to_right.wait_recv)
    pl.when(has["down"])(to_down[0].start)
    pl.when(has["up"])(to_up[0].start)
    pl.when(has["right"])(to_left.wait_recv)
    pl.when(has["down"])(to_down[2].start)
    pl.when(has["up"])(to_up[2].start)

    own = iota((A, A), 0) == iota((A, A), 1)
    scaled = [
        (jnp.concatenate([v.astype(F32)] * 2, axis=1) * factors).astype(BF16) for v in vectors
    ]
    scaled = jnp.concatenate(scaled, axis=0)
    products = []
    for c in range(3):
        diagonal = jnp.concatenate(
            [jnp.where(own, hess_ref[c, j, 0:1, :].astype(F32), 0.0).astype(BF16) for j in range(3)], axis=1
        )
        near = jnp.concatenate([w_local[c * 3 + j].T for j in range(3)], axis=1)
        products.append(dot(diagonal, scaled) + dot(near, scaled))
        wt_halo[c * A:(c + 1) * A, :] = jnp.concatenate([w_halo[c, b] for b in CORNERS], axis=0).T

    def far_rows(blocks):
        out = []
        for b in blocks:
            block = x_ref[b // 3, b % 3]
            packed = block[3 * H:]
            scale = jnp.concatenate([dot(packed, table), dot(packed, table_two)], axis=0)
            for j in range(3):
                rows = block[j * H:(j + 1) * H].astype(F32)
                out.append((jnp.concatenate([rows, rows], axis=1) * scale).astype(BF16))
        return jnp.concatenate(out, axis=0)

    for name, copies in (("up", to_down), ("down", to_up)):
        pl.when(has[name])(copies[1].wait_recv)
    edge_rows = far_rows(EDGES)
    for c in range(3):
        edges = jnp.concatenate([w_halo[c, b] for b in EDGES], axis=0).T
        products[c] += dot(edges, edge_rows)
    early = jnp.concatenate(products, axis=0)
    all_factors = jnp.concatenate([factors] * 3, axis=0)
    first_high, first_low = split(early * all_factors)
    first_gram = dot(turned, first_high) + dot(turned, first_low)
    corner_weights = wt_halo[...]
    corner_left = []
    for iso in range(2):
        scale = jnp.concatenate([all_factors[:, iso * V:(iso + 1) * V]] * 3, axis=1)
        high, low = split(corner_weights.astype(F32) * scale)
        corner_left.append(split(dot(turned, high) + dot(turned, low)))

    for name, copies in (("up", to_down), ("down", to_up)):
        @pl.when(has[name])
        def _():
            copies[0].wait_recv()
            copies[2].wait_recv()

    corner_rows = far_rows(CORNERS)
    rows = 2 * V // plane
    for iso in range(2):
        high, low = corner_left[iso]
        right = corner_rows[:, iso * V:(iso + 1) * V]
        gram = first_gram[:, iso * V:(iso + 1) * V] + (dot(high, right) + dot(low, right))
        g_ref[iso * (plane // 2):(iso + 1) * (plane // 2)] = gram.reshape(plane // 2, rows, V)

    def scatter(d):
        device, target = plane_device(d)
        pltpu.make_async_remote_copy(
            src_ref=g_ref.at[target], dst_ref=first_ref.at[back(d) - 1],
            send_sem=send_sem.at[0], recv_sem=recv_sem.at[0],
            device_id=device, device_id_type=MESH,
        ).start()

    def ring(distance, size):
        return min(distance % size, -distance % size)

    plane_order = sorted(
        range(1, plane), key=lambda d: -ring(d // per_z, n_x) - ring(d // 2 % n_y, n_y)
    )
    z_order = sorted(range(1, along), key=lambda d: -ring(d, along))
    for d in plane_order:
        scatter(d)

    def arrived(ref, number):
        pltpu.make_async_copy(ref, ref, recv_sem.at[number]).wait()

    def sent(ref, number):
        pltpu.make_async_copy(ref, ref, send_sem.at[number]).wait()

    product = early + dot(corner_weights, corner_rows)
    image_high, image_low = split(product * all_factors)
    rotations = [split(rot_ref[iso]) for iso in range(2)]
    for iso in range(2):
        high, low = image_high[:, iso * V:(iso + 1) * V], image_low[:, iso * V:(iso + 1) * V]
        r_high, r_low = rotations[iso]
        turned_ref[iso] = dot(high, r_high) + (dot(high, r_low) + dot(low, r_high))

    arrived(first_ref, 0)
    part_ref[0] = g_ref[in_plane] + jnp.sum(first_ref[...], axis=0)

    def exchange(d):
        pltpu.make_async_remote_copy(
            src_ref=part_ref.at[0], dst_ref=second_ref.at[along - 1 - d],
            send_sem=send_sem.at[1], recv_sem=recv_sem.at[1],
            device_id=z_device(d), device_id_type=MESH,
        ).start()

    pl.semaphore_wait(relay_sem, 2)
    for d in z_order:
        exchange(d)
    arrived(second_ref, 1)
    atoms_all = 3.0 * A * n_wide * n_narrow
    total = (part_ref[0] + jnp.sum(second_ref[...], axis=0)) / atoms_all
    sent(first_ref, 0)
    final_ref = part_ref.at[1]
    final_ref[...] = total

    def gather(d):
        device, _ = plane_device(d)
        pltpu.make_async_remote_copy(
            src_ref=final_ref, dst_ref=gram_ref.at[in_plane],
            send_sem=send_sem.at[2], recv_sem=recv_sem.at[2],
            device_id=device, device_id_type=MESH,
        ).start()

    for d in plane_order:
        gather(d)
    gram_ref[in_plane] = total
    arrived(first_ref, 2)
    sent(second_ref, 1)
    sent(first_ref, 2)
    pl.when(has["right"])(to_right.wait_send)
    pl.when(has["left"])(to_left.wait_send)
    for name, copies in (("down", to_down), ("up", to_up)):
        @pl.when(has[name])
        def _():
            for copy in copies:
                copy.wait_send()


def finish(gram_ref, turned_ref, vec_ref, rot_ref, gram_out, out_ref, rotated_ref, sem):
    stores = [pltpu.make_async_copy(gram_ref, gram_out, sem.at[2])]
    stores[0].start()
    half = gram_ref.shape[0] // 2
    for iso in range(2):
        high, low = split(gram_ref[iso * half:(iso + 1) * half].reshape(V, V))
        r_high, r_low = split(rot_ref[iso])
        m_high, m_low = split(dot(high, r_high) + (dot(high, r_low) + dot(low, r_high)))
        vectors = vec_ref[...].reshape(3 * A, V)
        rotated_ref[iso] = (
            turned_ref[iso] - (dot(vectors, m_high) + dot(vectors, m_low))
        ).astype(BF16).reshape(3, A, V)
        stores.append(pltpu.make_async_copy(rotated_ref.at[iso], out_ref.at[iso], sem.at[iso]))
        stores[-1].start()
    for store in stores:
        store.wait()


def local(n_wide, n_narrow, per_z, z_high, vectors, hessian, neighbours, halo_atoms, labels, masses, rotation):
    plane = per_z * (n_narrow // z_high)
    along = (n_wide // per_z) * z_high
    rows = 2 * V // plane
    vmem = pl.BlockSpec(memory_space=pltpu.VMEM)
    gram, turned = pl.pallas_call(
        functools.partial(kernel, n_wide, n_narrow, per_z, z_high),
        out_shape=(
            pltpu.VMEM((plane, rows, V), F32),
            pltpu.VMEM((2, 3 * A, V), F32),
        ),
        in_specs=[pl.BlockSpec(memory_space=pltpu.HBM)] * 7,
        out_specs=(vmem, vmem),
        scratch_shapes=[
            pltpu.VMEM((3, A, V), BF16),
            pltpu.VMEM((3, 3, 1 + K, A), BF16),
            pltpu.VMEM((K, A), jnp.int32),
            pltpu.VMEM((1, H), jnp.int32),
            pltpu.VMEM((1, A), jnp.int32),
            pltpu.VMEM((2, NISO), F32),
            pltpu.VMEM((2, V, V), F32),
            pltpu.VMEM((3, 3, PAY, V), BF16),
            pltpu.VMEM((128, A), F32),
            pltpu.VMEM((9, 128, A), F32),
            pltpu.VMEM((64, 16, A), BF16),
            pltpu.VMEM((9, 64, 16, A), BF16),
            pltpu.VMEM((9, A, A), BF16),
            pltpu.VMEM((3, 9, 3 * H, A), BF16),
            pltpu.VMEM((3 * A, 12 * H), BF16),
            pltpu.VMEM((plane, rows, V), F32),
            pltpu.VMEM((plane - 1, rows, V), F32),
            pltpu.VMEM((2, rows, V), F32),
            pltpu.VMEM((along - 1, rows, V), F32),
            pltpu.SemaphoreType.DMA((7,)),
            pltpu.SemaphoreType.DMA((9,)),
            pltpu.SemaphoreType.DMA((9,)),
            pltpu.SemaphoreType.DMA((3,)),
            pltpu.SemaphoreType.DMA((3,)),
            pltpu.SemaphoreType.REGULAR,
        ],
        compiler_params=pltpu.CompilerParams(
            collective_id=0, has_side_effects=True, vmem_limit_bytes=60 * 1024 * 1024
        ),
    )(vectors, hessian, neighbours, halo_atoms.reshape(1, H), labels.reshape(1, A), masses, rotation)
    anywhere = pl.BlockSpec(memory_space=pl.ANY)
    gram, rotated = pl.pallas_call(
        finish,
        out_shape=(
            jax.ShapeDtypeStruct((plane, rows, V), F32),
            jax.ShapeDtypeStruct((2, 3, A, V), BF16),
        ),
        in_specs=[vmem] * 4,
        out_specs=(anywhere, anywhere),
        scratch_shapes=[
            pltpu.VMEM((2, 3, A, V), BF16),
            pltpu.SemaphoreType.DMA((3,)),
        ],
        compiler_params=pltpu.CompilerParams(vmem_limit_bytes=8 * 1024 * 1024),
    )(gram, turned, vectors, rotation)
    return gram.reshape(2, V, V), rotated


def solution(mesh):
    n_wide, n_narrow = mesh.shape["wide"], mesh.shape["narrow"]
    per_z = n_wide // 4 if n_wide >= 16 else n_wide // 2
    z_high = 4 if n_narrow >= 16 else n_narrow // 2
    spread = ("wide", "narrow")
    return jax.shard_map(
        functools.partial(local, n_wide, n_narrow, per_z, z_high),
        mesh=mesh,
        in_specs=(
            P(None, spread, None),
            P(None, None, None, spread),
            P(None, spread),
            P(spread),
            P(spread),
            P(),
            P(),
        ),
        out_specs=(P(), P(None, None, spread, None)),
        check_vma=False,
    )
```

```python
import functools

import jax
import jax.numpy as jnp
from jax import lax
from jax.experimental import pallas as pl
from jax.experimental.pallas import tpu as pltpu
from jax.sharding import PartitionSpec as P

MESH = pl.DeviceIdType.MESH
F32 = jnp.float32
BF16 = jnp.bfloat16
A = 128
H = 32
V = 128
K = 60
UNROLL = 30
ROWS = A + 9 * H
NISO = 16
CORNERS, EDGES = (0, 6, 2, 8), (1, 3, 4, 5, 7)
PAY = 3 * H + H // 2
CENTRE = ROWS // 2


def dot(x, y, dims=((1,), (0,))):
    return lax.dot_general(x, y, (dims, ((), ())), preferred_element_type=F32)


def split(x):
    high = x.astype(BF16)
    return high, (x - high.astype(F32)).astype(BF16)


def iota(shape, dim):
    return lax.broadcasted_iota(jnp.int32, shape, dim)


def combine_duplicates(nbr_ref, hess_ref, nbr_pad, h_pad, nbr_x, h_x):
    nbr_pad[0:64, :] = jnp.full((64, A), -1.0, F32)
    nbr_pad[64:64 + K, :] = nbr_ref[...].astype(F32)
    nbr_pad[64 + K:128, :] = jnp.full((64 - K, A), -2.0, F32)
    for cj in range(9):
        h_pad[cj, 0:64, :] = jnp.zeros((64, A), F32)
        h_pad[cj, 64:64 + K, :] = hess_ref[cj // 3, cj % 3, 1:1 + K, :].astype(F32)
        h_pad[cj, 64 + K:128, :] = jnp.zeros((64 - K, A), F32)

    def eight_slots(m, _):
        first = 64 + 8 * m
        here = nbr_pad[pl.ds(first, 8), :]
        sums = tuple(h_pad[cj, pl.ds(first, 8), :] for cj in range(9))

        def eight_shifts(g, sums):
            for t in range(8):
                back = first - (8 * g + t + 1)
                same = nbr_pad[pl.ds(back, 8), :] == here
                sums = tuple(
                    s + jnp.where(same, h_pad[cj, pl.ds(back, 8), :], 0.0) for cj, s in enumerate(sums)
                )
            return sums

        sums = lax.fori_loop(0, m + 1, eight_shifts, sums)
        for t in range(8):
            nbr_x[8 * m + t] = jnp.broadcast_to(here[t:t + 1, :] - CENTRE, (16, A)).astype(BF16)
            for cj in range(9):
                h_x[cj, 8 * m + t] = jnp.broadcast_to(sums[cj][t:t + 1, :], (16, A)).astype(BF16)
        return 0

    lax.fori_loop(0, 8, eight_slots, 0)


def weight_rows(block, nbr_x, h_x):
    ids = (iota((16, A), 0) + (block * 32 - CENTRE)).astype(F32)
    low, high = ids.astype(BF16), (ids + 16.0).astype(BF16)
    zero = jnp.zeros((16, A), BF16)

    def many_slots(g, sums):
        for t in range(UNROLL):
            k = g * UNROLL + t
            row = nbr_x[k]
            at_low, at_high = row == low, row == high
            out = []
            for cj in range(9):
                value = h_x[cj, k]
                out.append(jnp.where(at_low, value, sums[2 * cj]))
                out.append(jnp.where(at_high, value, sums[2 * cj + 1]))
            sums = tuple(out)
        return sums

    return lax.fori_loop(0, K // UNROLL, many_slots, (zero,) * 18)


def kernel(
    n_wide, n_narrow, per_z, z_high,
    vec_in, hess_in, nbr_in, halo_in, lab_in, mass_in, rot_in,
    gram_ref, turned_ref,
    vec_ref, hess_ref, nbr_ref, halo_ref, lab_ref, mass_ref, rot_ref,
    x_ref, nbr_pad, h_pad, nbr_x, h_x, w_local, w_halo, wt_halo, g_ref, first_ref, part_ref, second_ref,
    load_sem, halo_send, halo_recv, send_sem, recv_sem, relay_sem,
):
    p, q = lax.axis_index("wide"), lax.axis_index("narrow")
    z_low = n_wide // per_z
    n_x = n_narrow // z_high
    plane, along = per_z * n_x, z_low * z_high
    in_plane = lax.div(q, z_high) * per_z + lax.rem(p, per_z)
    in_z = lax.rem(q, z_high) * z_low + lax.div(p, per_z)

    n_y = per_z // 2
    x_at, y_at, core = lax.div(q, z_high), lax.div(lax.rem(p, per_z), 2), lax.rem(p, 2)
    p_plane, q_plane = p - lax.rem(p, per_z), lax.rem(q, z_high)
    p_z, q_z = lax.rem(p, per_z), q - lax.rem(q, z_high)
    xs = [lax.rem(x_at + d, n_x) for d in range(n_x)]
    ys = [lax.rem(y_at + d, n_y) * 2 for d in range(n_y)]
    cores = [core, 1 - core]
    tops = [q_plane + x * z_high for x in xs]
    lows = [[y + c for c in cores] for y in ys]

    def plane_device(d):
        dx, dy, dc = d // per_z, d // 2 % n_y, d % 2
        return (p_plane + lows[dy][dc], tops[dx]), xs[dx] * per_z + lows[dy][dc]

    def z_device(d):
        at = lax.rem(in_z + d, along)
        return lax.rem(at, z_low) * per_z + p_z, q_z + lax.div(at, z_low)

    def back(d):
        dx, dy, dc = d // per_z, d // 2 % n_y, d % 2
        return (-dx % n_x) * per_z + (-dy % n_y) * 2 + dc

    has = {"up": p > 0, "down": p < n_wide - 1, "left": q > 0, "right": q < n_narrow - 1}
    where = {"up": (p - 1, q), "down": (p + 1, q), "left": (p, q - 1), "right": (p, q + 1)}

    for name, index in (("left", 0), ("right", 2)):
        @pl.when(jnp.logical_not(has[name]))
        def _():
            x_ref[1, index] = jnp.zeros((PAY, V), BF16)
    for name, index in (("up", 0), ("down", 2)):
        @pl.when(jnp.logical_not(has[name]))
        def _():
            x_ref[index] = jnp.zeros((3, PAY, V), BF16)

    barrier = pltpu.get_barrier_semaphore()

    def greet(device):
        pl.semaphore_signal(barrier, inc=1, device_id=device, device_id_type=MESH)

    for name in has:
        @pl.when(has[name])
        def _():
            greet(where[name])

    reach = along // 4
    for d in range(reach, 0, -1):
        greet(z_device(d))
        greet(z_device(along - d))
    for d in range(1, plane):
        greet(plane_device(d)[0])

    loads = [
        pltpu.make_async_copy(source, target, load_sem.at[number])
        for number, (source, target) in enumerate((
            (halo_in, halo_ref), (lab_in, lab_ref), (mass_in, mass_ref), (vec_in, vec_ref),
            (nbr_in, nbr_ref), (hess_in, hess_ref), (rot_in, rot_ref),
        ))
    ]
    for load in loads:
        load.start()
    for load in loads[:4]:
        load.wait()

    masses = mass_ref[...]
    roots = lax.rsqrt(masses)
    roots = roots * (1.5 - 0.5 * masses * roots * roots)
    pick = lax.rem(iota((A, NISO), 0), NISO) == iota((A, NISO), 1)
    group = iota((A, V), 0)
    table = []
    for iso in range(2):
        column = jnp.sum(jnp.where(pick, roots[iso:iso + 1, :], 0.0), axis=1, keepdims=True)
        full = jnp.broadcast_to(column, (A, V))
        one = full.astype(BF16).astype(F32)
        two = (full - one).astype(BF16).astype(F32)
        three = full - one - two
        table.append(
            jnp.where(group < 16, one, jnp.where(group < 32, two, jnp.where(group < 48, three, 0.0))).astype(BF16)
        )
    table = jnp.concatenate(table, axis=1)
    table_two = jnp.concatenate([jnp.zeros((V // 2, 2 * V), BF16), table[:V // 2]], axis=0)
    half = lax.rem(group, V // 2)
    classes = jnp.where(
        (lax.rem(group, NISO) == lab_ref[...]) & (half < 3 * NISO), 1.0, 0.0
    ).T.astype(BF16)
    factors = dot(classes, table)

    boundary = jnp.where(iota((A, H), 0) == halo_ref[...], 1.0, 0.0).astype(BF16)
    for j in range(3):
        x_ref[1, 1, j * H:(j + 1) * H, :] = dot(boundary, vec_ref[j], ((0,), (0,))).astype(BF16)
    chosen = dot(boundary, classes, ((0,), (0,)))
    x_ref[1, 1, 3 * H:, :] = jnp.where(
        iota((H // 2, V), 1) < V // 2, chosen[:H // 2], chosen[H // 2:]
    ).astype(BF16)

    for load in loads[4:]:
        load.wait()
    vectors = [vec_ref[j] for j in range(3)]
    stacked = vec_ref[...].reshape(3 * A, V)
    turned = stacked.astype(F32).T.astype(BF16)

    combine_duplicates(nbr_ref, hess_ref, nbr_pad, h_pad, nbr_x, h_x)

    def local_block(block, _):
        rows = weight_rows(block, nbr_x, h_x)
        for cj in range(9):
            at = pl.multiple_of(block * 32, 32)
            w_local[cj, pl.ds(at, 16), :] = rows[2 * cj]
            w_local[cj, pl.ds(pl.multiple_of(at + 16, 16), 16), :] = rows[2 * cj + 1]
        return 0

    lax.fori_loop(0, 2, local_block, 0)

    greetings = plane - 1 + 2 * reach
    for name in has:
        greetings = greetings + has[name].astype(jnp.int32)
    pl.semaphore_wait(barrier, greetings)

    def halo_copy(j, at, name):
        number = at[0] * 3 + at[1]
        return pltpu.make_async_remote_copy(
            src_ref=x_ref.at[1, j], dst_ref=x_ref.at[at[0], at[1]],
            send_sem=halo_send.at[number], recv_sem=halo_recv.at[number],
            device_id=where[name], device_id_type=MESH,
        )

    to_right, to_left = halo_copy(1, (1, 0), "right"), halo_copy(1, (1, 2), "left")
    to_down = [halo_copy(j, (0, j), "down") for j in range(3)]
    to_up = [halo_copy(j, (2, j), "up") for j in range(3)]
    pl.when(has["right"])(to_right.start)
    pl.when(has["left"])(to_left.start)
    pl.when(has["down"])(to_down[1].start)
    pl.when(has["up"])(to_up[1].start)

    for d in (reach, along - reach):
        pl.semaphore_signal(relay_sem, inc=1, device_id=z_device(d), device_id_type=MESH)

    def halo_block(block, _):
        rows = weight_rows(block + A // 32, nbr_x, h_x)
        for cj in range(9):
            at = (cj % 3) * H
            w_halo[cj // 3, block, at:at + 16, :] = rows[2 * cj]
            w_halo[cj // 3, block, at + 16:at + 32, :] = rows[2 * cj + 1]
        return 0

    lax.fori_loop(2, A // 32, local_block, 0)
    lax.fori_loop(0, 9, halo_block, 0)

    pl.when(has["left"])(to_right.wait_recv)
    pl.when(has["down"])(to_down[0].start)
    pl.when(has["up"])(to_up[0].start)
    pl.when(has["right"])(to_left.wait_recv)
    pl.when(has["down"])(to_down[2].start)
    pl.when(has["up"])(to_up[2].start)

    own = iota((A, A), 0) == iota((A, A), 1)
    scaled = [
        (jnp.concatenate([v.astype(F32)] * 2, axis=1) * factors).astype(BF16) for v in vectors
    ]
    scaled = jnp.concatenate(scaled, axis=0)
    products = []
    for c in range(3):
        diagonal = jnp.concatenate(
            [jnp.where(own, hess_ref[c, j, 0:1, :].astype(F32), 0.0).astype(BF16) for j in range(3)], axis=1
        )
        near = jnp.concatenate([w_local[c * 3 + j].T for j in range(3)], axis=1)
        products.append(dot(diagonal, scaled) + dot(near, scaled))
        wt_halo[c * A:(c + 1) * A, :] = jnp.concatenate([w_halo[c, b] for b in CORNERS], axis=0).T

    def far_rows(blocks):
        out = []
        for b in blocks:
            block = x_ref[b // 3, b % 3]
            packed = block[3 * H:]
            scale = jnp.concatenate([dot(packed, table), dot(packed, table_two)], axis=0)
            for j in range(3):
                rows = block[j * H:(j + 1) * H].astype(F32)
                out.append((jnp.concatenate([rows, rows], axis=1) * scale).astype(BF16))
        return jnp.concatenate(out, axis=0)

    for name, copies in (("up", to_down), ("down", to_up)):
        pl.when(has[name])(copies[1].wait_recv)
    edge_rows = far_rows(EDGES)
    for c in range(3):
        edges = jnp.concatenate([w_halo[c, b] for b in EDGES], axis=0).T
        products[c] += dot(edges, edge_rows)
    early = jnp.concatenate(products, axis=0)
    all_factors = jnp.concatenate([factors] * 3, axis=0)
    first_high, first_low = split(early * all_factors)
    first_gram = dot(turned, first_high) + dot(turned, first_low)
    corner_weights = wt_halo[...]
    corner_left = []
    for iso in range(2):
        scale = jnp.concatenate([all_factors[:, iso * V:(iso + 1) * V]] * 3, axis=1)
        high, low = split(corner_weights.astype(F32) * scale)
        left = split(dot(turned, high) + dot(turned, low))
        corner_left.append([[part[:, :6 * H] for part in left], [part[:, 6 * H:] for part in left]])

    grams = [first_gram[:, iso * V:(iso + 1) * V] for iso in range(2)]
    corner_rows = []
    for side in range(2):
        for name, copies in (("up", to_down), ("down", to_up)):
            pl.when(has[name])(copies[2 * side].wait_recv)
        corner_rows.append(far_rows(CORNERS[2 * side:2 * side + 2]))
        for iso in range(2):
            high, low = corner_left[iso][side]
            right = corner_rows[side][:, iso * V:(iso + 1) * V]
            grams[iso] += dot(high, right) + dot(low, right)
    corner_rows = jnp.concatenate(corner_rows, axis=0)
    rows = 2 * V // plane
    for iso in range(2):
        g_ref[iso * (plane // 2):(iso + 1) * (plane // 2)] = grams[iso].reshape(plane // 2, rows, V)

    def scatter(d):
        device, target = plane_device(d)
        pltpu.make_async_remote_copy(
            src_ref=g_ref.at[target], dst_ref=first_ref.at[back(d) - 1],
            send_sem=send_sem.at[0], recv_sem=recv_sem.at[0],
            device_id=device, device_id_type=MESH,
        ).start()

    def ring(distance, size):
        return min(distance % size, -distance % size)

    plane_order = sorted(
        range(1, plane), key=lambda d: -ring(d // per_z, n_x) - ring(d // 2 % n_y, n_y)
    )
    z_order = sorted(range(1, along), key=lambda d: -ring(d, along))
    for d in plane_order:
        scatter(d)

    def arrived(ref, number):
        pltpu.make_async_copy(ref, ref, recv_sem.at[number]).wait()

    def sent(ref, number):
        pltpu.make_async_copy(ref, ref, send_sem.at[number]).wait()

    product = early + dot(corner_weights, corner_rows)
    image_high, image_low = split(product * all_factors)
    rotations = [split(rot_ref[iso]) for iso in range(2)]
    for iso in range(2):
        high, low = image_high[:, iso * V:(iso + 1) * V], image_low[:, iso * V:(iso + 1) * V]
        r_high, r_low = rotations[iso]
        turned_ref[iso] = dot(high, r_high) + (dot(high, r_low) + dot(low, r_high))

    arrived(first_ref, 0)
    part_ref[0] = g_ref[in_plane] + jnp.sum(first_ref[...], axis=0)

    def exchange(d):
        pltpu.make_async_remote_copy(
            src_ref=part_ref.at[0], dst_ref=second_ref.at[along - 1 - d],
            send_sem=send_sem.at[1], recv_sem=recv_sem.at[1],
            device_id=z_device(d), device_id_type=MESH,
        ).start()

    pl.semaphore_wait(relay_sem, 2)
    for d in z_order:
        exchange(d)
    arrived(second_ref, 1)
    atoms_all = 3.0 * A * n_wide * n_narrow
    total = (part_ref[0] + jnp.sum(second_ref[...], axis=0)) / atoms_all
    sent(first_ref, 0)
    final_ref = part_ref.at[1]
    final_ref[...] = total

    def gather(d):
        device, _ = plane_device(d)
        pltpu.make_async_remote_copy(
            src_ref=final_ref, dst_ref=gram_ref.at[in_plane],
            send_sem=send_sem.at[2], recv_sem=recv_sem.at[2],
            device_id=device, device_id_type=MESH,
        ).start()

    for d in plane_order:
        gather(d)
    gram_ref[in_plane] = total
    arrived(first_ref, 2)
    sent(second_ref, 1)
    sent(first_ref, 2)
    pl.when(has["right"])(to_right.wait_send)
    pl.when(has["left"])(to_left.wait_send)
    for name, copies in (("down", to_down), ("up", to_up)):
        @pl.when(has[name])
        def _():
            for copy in copies:
                copy.wait_send()


def finish(gram_ref, turned_ref, vec_ref, rot_ref, gram_out, out_ref, rotated_ref, sem):
    stores = [pltpu.make_async_copy(gram_ref, gram_out, sem.at[2])]
    stores[0].start()
    half = gram_ref.shape[0] // 2
    for iso in range(2):
        high, low = split(gram_ref[iso * half:(iso + 1) * half].reshape(V, V))
        r_high, r_low = split(rot_ref[iso])
        m_high, m_low = split(dot(high, r_high) + (dot(high, r_low) + dot(low, r_high)))
        vectors = vec_ref[...].reshape(3 * A, V)
        rotated_ref[iso] = (
            turned_ref[iso] - (dot(vectors, m_high) + dot(vectors, m_low))
        ).astype(BF16).reshape(3, A, V)
        stores.append(pltpu.make_async_copy(rotated_ref.at[iso], out_ref.at[iso], sem.at[iso]))
        stores[-1].start()
    for store in stores:
        store.wait()


def local(n_wide, n_narrow, per_z, z_high, vectors, hessian, neighbours, halo_atoms, labels, masses, rotation):
    plane = per_z * (n_narrow // z_high)
    along = (n_wide // per_z) * z_high
    rows = 2 * V // plane
    vmem = pl.BlockSpec(memory_space=pltpu.VMEM)
    gram, turned = pl.pallas_call(
        functools.partial(kernel, n_wide, n_narrow, per_z, z_high),
        out_shape=(
            pltpu.VMEM((plane, rows, V), F32),
            pltpu.VMEM((2, 3 * A, V), F32),
        ),
        in_specs=[pl.BlockSpec(memory_space=pltpu.HBM)] * 7,
        out_specs=(vmem, vmem),
        scratch_shapes=[
            pltpu.VMEM((3, A, V), BF16),
            pltpu.VMEM((3, 3, 1 + K, A), BF16),
            pltpu.VMEM((K, A), jnp.int32),
            pltpu.VMEM((1, H), jnp.int32),
            pltpu.VMEM((1, A), jnp.int32),
            pltpu.VMEM((2, NISO), F32),
            pltpu.VMEM((2, V, V), F32),
            pltpu.VMEM((3, 3, PAY, V), BF16),
            pltpu.VMEM((128, A), F32),
            pltpu.VMEM((9, 128, A), F32),
            pltpu.VMEM((64, 16, A), BF16),
            pltpu.VMEM((9, 64, 16, A), BF16),
            pltpu.VMEM((9, A, A), BF16),
            pltpu.VMEM((3, 9, 3 * H, A), BF16),
            pltpu.VMEM((3 * A, 12 * H), BF16),
            pltpu.VMEM((plane, rows, V), F32),
            pltpu.VMEM((plane - 1, rows, V), F32),
            pltpu.VMEM((2, rows, V), F32),
            pltpu.VMEM((along - 1, rows, V), F32),
            pltpu.SemaphoreType.DMA((7,)),
            pltpu.SemaphoreType.DMA((9,)),
            pltpu.SemaphoreType.DMA((9,)),
            pltpu.SemaphoreType.DMA((3,)),
            pltpu.SemaphoreType.DMA((3,)),
            pltpu.SemaphoreType.REGULAR,
        ],
        compiler_params=pltpu.CompilerParams(
            collective_id=0, has_side_effects=True, vmem_limit_bytes=60 * 1024 * 1024
        ),
    )(vectors, hessian, neighbours, halo_atoms.reshape(1, H), labels.reshape(1, A), masses, rotation)
    anywhere = pl.BlockSpec(memory_space=pl.ANY)
    gram, rotated = pl.pallas_call(
        finish,
        out_shape=(
            jax.ShapeDtypeStruct((plane, rows, V), F32),
            jax.ShapeDtypeStruct((2, 3, A, V), BF16),
        ),
        in_specs=[vmem] * 4,
        out_specs=(anywhere, anywhere),
        scratch_shapes=[
            pltpu.VMEM((2, 3, A, V), BF16),
            pltpu.SemaphoreType.DMA((3,)),
        ],
        compiler_params=pltpu.CompilerParams(vmem_limit_bytes=8 * 1024 * 1024),
    )(gram, turned, vectors, rotation)
    return gram.reshape(2, V, V), rotated


def solution(mesh):
    n_wide, n_narrow = mesh.shape["wide"], mesh.shape["narrow"]
    per_z = n_wide // 4 if n_wide >= 16 else n_wide // 2
    z_high = 4 if n_narrow >= 16 else n_narrow // 2
    spread = ("wide", "narrow")
    return jax.shard_map(
        functools.partial(local, n_wide, n_narrow, per_z, z_high),
        mesh=mesh,
        in_specs=(
            P(None, spread, None),
            P(None, None, None, spread),
            P(None, spread),
            P(spread),
            P(spread),
            P(),
            P(),
        ),
        out_specs=(P(), P(None, None, spread, None)),
        check_vma=False,
    )
```
